32 devices in a mesh: seq: 8 (over z, core), img: 4 (over y, x).
Axes of the slice: x: 2, y: 2, z: 4, core: 2. Of those that a mesh axis runs over, the one named last changes fastest.
Arguments:
- tokens: bfloat16 [4, 24, 128, 2240], P('img', 'seq'), may hold values from -8 to 8
- norm_gain: bfloat16 [2240], replicated, may hold values from 0.099609375 to 1.8984375
- caption: bfloat16 [4, 2240], P('img'), may hold values from -6 to 6
- null_caption: bfloat16 [2240], replicated, may hold values from -6 to 6
- keep: int32 [4], P('img'), may hold values from 0 to 1, as said below
- bucket_rows: int32 [4], P('img'), may hold values from 7 to 24, as said below
- w_qkv: bfloat16 [2240, 3456], P('img', 'seq'), may hold values from -0.125 to 0.125
Outputs:
- attended: bfloat16 [4, 24, 128, 1152], P('img', 'seq')
The draws below stay inside these ranges and needn't reach their ends.
Inputs may be any that keep to these rules, and one draw needn't show every extreme that they name: `keep`: 1 keeps the image's caption, 0 drops it; some image keeps and some drops. `bucket_rows`: rows in use are the first ones of an image's grid; some image uses all 24 rows.
All inputs are finite; a program needn't handle non-finite values.
Results may differ from the reference program's by a relative error of at most 0.0017.
Values may be sent and summed in bfloat16 or wider, within the bound.
A program may use at most 128 MiB of HBM per device.

```python
import jax
import jax.numpy as jnp
from jax import lax

D = 2240
HDIM = 32
HEADS = 36
WID = 128
INNER = 1152
HGT = 24
NIMG = 4


def draw_tokens(key, part):
    first, second = jax.random.split(key, 2)
    noise = jax.random.normal(first, (NIMG, HGT, WID, D), jnp.float32)
    means = jax.random.normal(second, (NIMG, HGT, 1, D), jnp.float32)
    values = noise + means
    return jnp.clip(values, -8.0, 8.0).astype(jnp.bfloat16)


def draw_keep(key, part):
    first, second = jax.random.split(jax.random.fold_in(key, 11))
    flags = jax.random.randint(first, (NIMG,), 0, 2)
    chosen = jax.random.randint(second, (), 0, NIMG)
    position = jnp.arange(NIMG, dtype=jnp.int32)
    flags = jnp.where(position == chosen, 1, flags)
    flags = jnp.where(position == (chosen + 1) % NIMG, 0, flags)
    return flags.astype(jnp.int32)


def draw_bucket_rows(key, part):
    first, second = jax.random.split(jax.random.fold_in(key, 23))
    lowest = HGT // 4 + 1
    heights = jax.random.randint(first, (NIMG,), lowest, HGT + 1)
    chosen = jax.random.randint(second, (), 0, NIMG)
    position = jnp.arange(NIMG, dtype=jnp.int32)
    heights = jnp.where(position == chosen, HGT, heights)
    heights = jnp.where(position == (chosen + 1) % NIMG, lowest, heights)
    return heights.astype(jnp.int32)


def block_levels(own_key, shape, shards, least, high):
    loudness = 1.0
    for axis_at, shards_of in shards:
        steps = jax.random.uniform(jax.random.fold_in(jax.random.fold_in(own_key, 6), axis_at), (shards_of,), jnp.float32, least / len(shards), high / len(shards))
        loudness = loudness * jnp.repeat(jnp.exp(steps), shape[axis_at] // shards_of).reshape((-1,) + (1,) * (len(shape) - 1 - axis_at))
    return loudness


def gaussian(stream_key, dims, scale, most, cuts=(), kind=jnp.bfloat16):
    values = scale * jax.random.normal(stream_key, dims, jnp.float32)
    if cuts:
        values = values * block_levels(stream_key, dims, cuts, -0.22, 0.18)
    return jnp.clip(values, -most, most).astype(kind)


def setup_inputs(seed: int = 0) -> dict:
    key_of = jax.random.split(jax.random.key(seed), 8)
    tokens = draw_tokens(jax.random.fold_in(key_of[7], 71), 0)
    norm_gain = jnp.clip(1.0 + 0.18 * jax.random.normal(key_of[1], (D,), jnp.float32), 0.099609375, 1.8984375).astype(jnp.bfloat16)
    caption = gaussian(key_of[2], (NIMG, D), 1.0, 6.0, ((0, 4),))
    null_caption = gaussian(key_of[3], (D,), 1.0, 6.0)
    keep = draw_keep(jax.random.fold_in(key_of[7], 71), 0)
    bucket_rows = draw_bucket_rows(jax.random.fold_in(key_of[7], 71), 0)
    w_qkv = gaussian(key_of[6], (D, 3 * INNER), D ** -0.5, 0.125, ((0, 4), (1, 8)))
    return dict(tokens=tokens, norm_gain=norm_gain, caption=caption, null_caption=null_caption, keep=keep, bucket_rows=bucket_rows, w_qkv=w_qkv)


norm_eps = 1e-06
attn_eps = 1e-06

def reference(tokens, norm_gain, caption, null_caption, keep, bucket_rows, w_qkv):
    inner_width = HEADS * HDIM
    token_count = HGT * WID

    def one_image(items):
        image, caption_row, keep_flag, height = items
        features = image.reshape(token_count, D).astype(jnp.float32)
        mean_square = lax.optimization_barrier(jnp.mean(features * features, axis=1, keepdims=True))
        condition = jnp.where(keep_flag > 0, caption_row, null_caption).astype(jnp.float32)
        hidden = (features * lax.rsqrt(mean_square + norm_eps) * norm_gain.astype(jnp.float32) + condition).astype(jnp.bfloat16)
        projected = jnp.dot(hidden, w_qkv, preferred_element_type=jnp.float32)
        grid_row = jnp.arange(token_count, dtype=jnp.int32) // WID
        live_mask = (grid_row < height).astype(jnp.float32)
        queries = jax.nn.relu(projected[:, :inner_width]).reshape(token_count, HEADS, HDIM)
        keys_relu = jax.nn.relu(projected[:, inner_width:2 * inner_width]).reshape(token_count, HEADS, HDIM)
        keys_relu = keys_relu * live_mask[:, None, None]
        values = projected[:, 2 * inner_width:].reshape(token_count, HEADS, HDIM)
        state_outer = jnp.einsum('thd,the->hde', keys_relu, values, precision=lax.Precision.HIGHEST)
        key_total = lax.optimization_barrier(jnp.sum(keys_relu, axis=0))
        numerator = jnp.einsum('thd,hde->the', queries, state_outer, precision=lax.Precision.HIGHEST)
        denominator = jnp.einsum('thd,hd->th', queries, key_total, precision=lax.Precision.HIGHEST)
        result = numerator / (denominator[:, :, None] + attn_eps) * live_mask[:, None, None]
        return result.reshape(HGT, WID, inner_width).astype(jnp.bfloat16)
    return lax.map(one_image, (tokens, caption, keep, bucket_rows))
```

```python
import functools

import jax
import jax.numpy as jnp
from jax import lax
from jax.experimental import pallas as pl
from jax.experimental.pallas import tpu as pltpu
from jax.sharding import PartitionSpec as P

HDIM = 32
LANES = 128
PARTS = 2

norm_eps = 1e-06
attn_eps = 1e-06
HIGHEST = lax.Precision.HIGHEST


def gray(r):
    return r + r // 2 - 2 * (r // 3)


def kernel(
    dims,
    tokens_ref, gain_ref, caption_ref, null_ref, keep_ref, rows_ref, w_ref,
    out_ref,
    own, wbuf, hid, proj, full, state, pieces, total,
    send_sems, z_sems, left_sems, right_sems, far_sems, twin_sems, piece_sems, total_sems, local_sem,
):
    n_img, n_seq, grid_rows, grid_cols, depth, width, inner = dims
    main_tiles = width // LANES
    main = main_tiles * LANES
    tail = width - main
    deep_tiles = -(-depth // LANES)
    packed = own.shape[0]
    part_rows = packed // PARTS
    n_z = n_seq // 2
    token_count = grid_rows * grid_cols

    seq = lax.axis_index("seq")
    img = lax.axis_index("img")
    core = lax.rem(seq, 2)
    z = seq // 2
    ring = gray(img)
    right = gray(lax.rem(ring + 1, 4))
    left = gray(lax.rem(ring + 3, 4))
    far = gray(lax.rem(ring + 2, 4))
    twin = seq + 1 - 2 * core
    zs = [z, z + 1 - 2 * lax.rem(z, 2), lax.rem(z + 2, 4), 3 - z]
    mine = [2 * q + core for q in zs]
    twins = [2 * q + 1 - core for q in zs]

    barrier = pltpu.get_barrier_semaphore()
    peers = [(img, lax.rem(seq + d, n_seq)) for d in range(1, n_seq)] + [(left, seq), (right, seq)]
    for i, s in peers:
        pl.semaphore_signal(
            barrier, inc=1, device_id={"img": i, "seq": s}, device_id_type=pl.DeviceIdType.MESH
        )

    for j in range(main_tiles):
        own[depth * j : depth * (j + 1), :] = w_ref[:, LANES * j : LANES * (j + 1)]
    rows_at = lax.broadcasted_iota(jnp.int32, (tail, tail), 0)
    cols_at = lax.broadcasted_iota(jnp.int32, (tail, tail), 1)
    unit = (rows_at == cols_at).astype(jnp.bfloat16)
    rest = lax.dot_general(
        unit, w_ref[:, main:width], (((1,), (1,)), ((), ())), preferred_element_type=jnp.float32
    ).astype(jnp.bfloat16)
    base = depth * main_tiles
    for j in range(deep_tiles):
        lanes = min(LANES, depth - LANES * j)
        if lanes < LANES:
            own[base + tail * j : base + tail * (j + 1), :] = jnp.zeros((tail, LANES), jnp.bfloat16)
        own[base + tail * j : base + tail * (j + 1), 0:lanes] = rest[:, LANES * j : LANES * j + lanes]

    pl.semaphore_wait(barrier, len(peers))

    sends = []

    def part(p):
        return pl.ds(p * part_rows, part_rows)

    def send(src, i, s, p, recv_sem, to_img, to_seq):
        copy = pltpu.make_async_remote_copy(
            src_ref=src,
            dst_ref=wbuf.at[i, s, part(p)],
            send_sem=send_sems.at[len(sends)],
            recv_sem=recv_sem,
            device_id={"img": to_img, "seq": to_seq},
            device_id_type=pl.DeviceIdType.MESH,
        )
        copy.start()
        sends.append(copy)

    def arrive(i, s, p, recv_sem):
        block = wbuf.at[i, s, part(p)]
        pltpu.make_async_remote_copy(
            src_ref=block, dst_ref=block, send_sem=send_sems.at[0], recv_sem=recv_sem,
            device_id={"img": img, "seq": twin}, device_id_type=pl.DeviceIdType.MESH,
        ).wait_recv()
        return block

    keep_own = pltpu.make_async_copy(own, wbuf.at[img, seq], local_sem)
    keep_own.start()
    for p in range(PARTS):
        src = own.at[part(p)]
        send(src, img, seq, p, left_sems.at[0, p], right, seq)
        send(src, img, seq, p, right_sems.at[0, p], left, seq)
        send(src, img, seq, p, z_sems.at[0, p], img, mine[1])
        send(src, img, seq, p, twin_sems.at[0, 0, p], img, twin)
    for k in range(2, n_z):
        for p in range(PARTS):
            send(own.at[part(p)], img, seq, p, z_sems.at[k - 1, p], img, mine[k])

    keep_flag = (keep_ref[0] > 0).astype(jnp.float32)
    condition = jnp.where(
        jnp.full((1, depth * n_img), keep_flag) > 0.5,
        caption_ref[...].astype(jnp.float32),
        null_ref[...].astype(jnp.float32),
    )
    gain = gain_ref[...].astype(jnp.float32)
    deep = deep_tiles * LANES
    if deep > depth:
        hid[:, :, deep - LANES :] = jnp.zeros((n_img, token_count, LANES), jnp.bfloat16)
    step_rows = 32

    @pl.loop(0, token_count // step_rows)
    def _(t):
        rows = pl.ds(pl.multiple_of(t * step_rows, step_rows), step_rows)
        features = tokens_ref[rows, :].astype(jnp.float32)
        mean_square = jnp.mean(features * features, axis=1, keepdims=True)
        hidden = (features * lax.rsqrt(mean_square + norm_eps) * gain + condition).astype(jnp.bfloat16)
        for i in range(n_img):
            hid[i, rows, 0:depth] = hidden[:, depth * i : depth * (i + 1)]

    keep_own.wait()

    def project(s):
        @pl.loop(0, grid_rows)
        def _(t):
            rows = pl.ds(pl.multiple_of(t * grid_cols, grid_cols), grid_cols)
            acc = jnp.zeros((grid_cols, main), jnp.float32)
            acc_tail = jnp.zeros((grid_cols, tail), jnp.float32)
            for i in range(n_img):
                block = jnp.concatenate(
                    [wbuf[i, s, depth * j : depth * (j + 1), :] for j in range(main_tiles)], axis=1
                )
                acc += jnp.dot(hid[i, rows, 0:depth], block, preferred_element_type=jnp.float32)
                ends = jnp.concatenate(
                    [wbuf[i, s, base + tail * j : base + tail * (j + 1), :] for j in range(deep_tiles)],
                    axis=1,
                )
                acc_tail += lax.dot_general(
                    hid[i, rows, :], ends, (((1,), (1,)), ((), ())), preferred_element_type=jnp.float32
                )
            proj[s, rows, 0:main] = acc
            proj[s, rows, main:width] = acc_tail

    def finish(k):
        for p in range(PARTS):
            for at, i in enumerate((img, left, right)):
                arrive(i, twins[k], p, twin_sems.at[k, at, p])
        arrive(far, twins[k], 0, twin_sems.at[k, 3, 0])
        arrive(far, twins[k], 1, twin_sems.at[k, 3, 1])
        project(mine[k])
        project(twins[k])

    for k in range(n_z):
        if k + 1 < n_z:
            s = mine[k + 1]
            for p in range(PARTS):
                src = arrive(img, s, p, z_sems.at[k, p])
                send(src, img, s, p, left_sems.at[k + 1, p], right, seq)
                send(src, img, s, p, right_sems.at[k + 1, p], left, seq)
                send(src, img, s, p, twin_sems.at[k + 1, 0, p], img, twin)
        s = mine[k]
        for p in range(PARTS):
            src = arrive(left, s, p, left_sems.at[k, p])
            if p == 0:
                send(src, left, s, p, far_sems.at[k, 0], right, seq)
            send(src, left, s, p, twin_sems.at[k, 1, p], img, twin)
            src = arrive(right, s, p, right_sems.at[k, p])
            if p == 1:
                send(src, right, s, p, far_sems.at[k, 1], left, seq)
            send(src, right, s, p, twin_sems.at[k, 2, p], img, twin)
        if k > 0:
            finish(k - 1)
        for p in range(PARTS):
            src = arrive(far, s, p, far_sems.at[k, p])
            send(src, far, s, p, twin_sems.at[k, 3, p], img, twin)
    finish(n_z - 1)

    @pl.loop(0, grid_rows)
    def _(t):
        rows = pl.ds(pl.multiple_of(t * grid_cols, grid_cols), grid_cols)
        for s in range(n_seq):
            full[rows, width * s : width * (s + 1)] = proj[s, rows, 0:width]

    groups = inner // LANES
    head_of_row = lax.broadcasted_iota(jnp.int32, (LANES, LANES), 0) // HDIM
    head_of_col = lax.broadcasted_iota(jnp.int32, (LANES, LANES), 1) // HDIM
    same = (head_of_row == head_of_col).astype(jnp.float32)
    live_rows = seq * grid_rows + lax.broadcasted_iota(jnp.int32, (token_count, LANES), 0) // grid_cols
    live = (live_rows < rows_ref[0]).astype(jnp.float32)
    state[...] = jnp.zeros_like(state)
    for g in range(groups):
        keys = jax.nn.relu(full[:, inner + LANES * g : inner + LANES * (g + 1)]) * live
        values = full[:, 2 * inner + LANES * g : 2 * inner + LANES * (g + 1)]
        outer = lax.dot_general(
            keys, values, (((0,), (0,)), ((), ())), precision=HIGHEST, preferred_element_type=jnp.float32
        ) * same
        state[HDIM * g : HDIM * (g + 1), :] = (
            outer[0:32] + outer[32:64] + outer[64:96] + outer[96:128]
        )
        state[HDIM * groups + g : HDIM * groups + g + 1, :] = jnp.sum(keys, axis=0, keepdims=True)

    piece = state.shape[0] // n_seq

    def piece_of(ref, s):
        return ref.at[pl.ds(pl.multiple_of(s * piece, piece), piece)]

    scattered, gathered = [], []
    for d in range(1, n_seq):
        to = lax.rem(seq + d, n_seq)
        copy = pltpu.make_async_remote_copy(
            src_ref=piece_of(state, to), dst_ref=pieces.at[d - 1],
            send_sem=send_sems.at[len(sends) + d - 1], recv_sem=piece_sems.at[d - 1],
            device_id={"img": img, "seq": to}, device_id_type=pl.DeviceIdType.MESH,
        )
        copy.start()
        scattered.append(copy)
    summed = state[pl.ds(pl.multiple_of(seq * piece, piece), piece), :]
    for d in range(1, n_seq):
        scattered[d - 1].wait_recv()
        summed = summed + pieces[d - 1]
    total[pl.ds(pl.multiple_of(seq * piece, piece), piece), :] = summed
    for d in range(1, n_seq):
        copy = pltpu.make_async_remote_copy(
            src_ref=piece_of(total, seq), dst_ref=piece_of(total, seq),
            send_sem=send_sems.at[len(sends) + n_seq - 1 + d - 1], recv_sem=total_sems.at[d - 1],
            device_id={"img": img, "seq": lax.rem(seq + d, n_seq)}, device_id_type=pl.DeviceIdType.MESH,
        )
        copy.start()
        gathered.append(copy)
    for d in range(1, n_seq):
        block = piece_of(total, lax.rem(seq + n_seq - d, n_seq))
        pltpu.make_async_remote_copy(
            src_ref=block, dst_ref=block, send_sem=send_sems.at[0], recv_sem=total_sems.at[d - 1],
            device_id={"img": img, "seq": twin}, device_id_type=pl.DeviceIdType.MESH,
        ).wait_recv()

    for g in range(groups):
        queries = jax.nn.relu(full[:, LANES * g : LANES * (g + 1)])
        compact = total[HDIM * g : HDIM * (g + 1), :]
        outer = jnp.concatenate([compact] * (LANES // HDIM), axis=0) * same
        key_total = total[HDIM * groups + g : HDIM * groups + g + 1, :]
        numerator = jnp.dot(queries, outer, precision=HIGHEST, preferred_element_type=jnp.float32)
        denominator = jnp.dot(
            queries * key_total, same, precision=HIGHEST, preferred_element_type=jnp.float32
        )
        out_ref[:, LANES * g : LANES * (g + 1)] = (
            numerator / (denominator + attn_eps) * live
        ).astype(out_ref.dtype)

    for copy in sends + scattered + gathered:
        copy.wait_send()


def fast_body(mesh, tokens, norm_gain, caption, null_caption, keep, bucket_rows, w_qkv):
    n_img, n_seq = mesh.shape["img"], mesh.shape["seq"]
    _, grid_rows, grid_cols, features = tokens.shape
    depth, width = w_qkv.shape
    inner = width * n_seq // 3
    token_count = grid_rows * grid_cols
    n_z = n_seq // 2
    tail = width % LANES
    deep_tiles = -(-depth // LANES)
    packed = depth * (width // LANES) + tail * deep_tiles
    state_rows = (HDIM + 1) * (inner // LANES)
    piece = -(-state_rows // (8 * n_seq)) * 8
    dims = (n_img, n_seq, grid_rows, grid_cols, depth, width, inner)
    vmem = pl.BlockSpec(memory_space=pltpu.VMEM)
    smem = pl.BlockSpec(memory_space=pltpu.SMEM)
    dma = pltpu.SemaphoreType.DMA
    out = pl.pallas_call(
        functools.partial(kernel, dims),
        out_shape=jax.ShapeDtypeStruct((token_count, inner), jnp.bfloat16),
        in_specs=[vmem, vmem, vmem, vmem, smem, smem, vmem],
        out_specs=vmem,
        scratch_shapes=[
            pltpu.VMEM((packed, LANES), jnp.bfloat16),
            pltpu.VMEM((n_img, n_seq, packed, LANES), jnp.bfloat16),
            pltpu.VMEM((n_img, token_count, deep_tiles * LANES), jnp.bfloat16),
            pltpu.VMEM((n_seq, token_count, -(-width // LANES) * LANES), jnp.float32),
            pltpu.VMEM((token_count, 3 * inner), jnp.float32),
            pltpu.VMEM((piece * n_seq, LANES), jnp.float32),
            pltpu.VMEM((n_seq - 1, piece, LANES), jnp.float32),
            pltpu.VMEM((piece * n_seq, LANES), jnp.float32),
            dma((96,)),
            dma((n_z - 1, PARTS)),
            dma((n_z, PARTS)),
            dma((n_z, PARTS)),
            dma((n_z, PARTS)),
            dma((n_z, 4, PARTS)),
            dma((n_seq - 1,)),
            dma((n_seq - 1,)),
            dma(()),
        ],
        compiler_params=pltpu.CompilerParams(
            collective_id=0, has_side_effects=True, vmem_limit_bytes=56 * 1024 * 1024
        ),
        cost_estimate=pl.CostEstimate(
            flops=2 * token_count * features * 3 * inner, bytes_accessed=4 * token_count * features,
            transcendentals=0,
        ),
    )(
        tokens.reshape(token_count, features), norm_gain.reshape(1, features), caption,
        null_caption.reshape(1, features), keep, bucket_rows, w_qkv,
    )
    return out.reshape(1, grid_rows, grid_cols, inner)


def body(tokens, norm_gain, caption, null_caption, keep, bucket_rows, w_qkv):
    grid_rows = tokens.shape[1]
    grid_cols = tokens.shape[2]
    features_count = tokens.shape[3]
    token_count = grid_rows * grid_cols
    features = tokens.reshape(token_count, features_count).astype(jnp.float32)
    mean_square = jnp.mean(features * features, axis=1, keepdims=True)
    condition = jnp.where(keep[0] > 0, caption[0], null_caption).astype(jnp.float32)
    hidden = (
        features * lax.rsqrt(mean_square + norm_eps) * norm_gain.astype(jnp.float32) + condition
    ).astype(jnp.bfloat16)
    rows_whole = lax.all_gather(w_qkv, "img", axis=0, tiled=True)
    projected = jnp.dot(
        hidden,
        lax.all_gather(rows_whole, "seq", axis=1, tiled=True),
        preferred_element_type=jnp.float32,
    )
    inner_width = projected.shape[1] // 3
    head_count = inner_width // HDIM
    grid_row = (
        lax.axis_index("seq") * grid_rows + jnp.arange(token_count, dtype=jnp.int32) // grid_cols
    )
    live_mask = (grid_row < bucket_rows[0]).astype(jnp.float32)
    queries = jax.nn.relu(projected[:, :inner_width]).reshape(token_count, head_count, HDIM)
    keys_relu = jax.nn.relu(projected[:, inner_width : 2 * inner_width]).reshape(
        token_count, head_count, HDIM
    )
    keys_relu = keys_relu * live_mask[:, None, None]
    values = projected[:, 2 * inner_width :].reshape(token_count, head_count, HDIM)
    state_outer = jnp.einsum("thd,the->hde", keys_relu, values, precision=lax.Precision.HIGHEST)
    key_total = jnp.sum(keys_relu, axis=0)
    state_outer, key_total = lax.psum((state_outer, key_total), "seq")
    numerator = jnp.einsum("thd,hde->the", queries, state_outer, precision=lax.Precision.HIGHEST)
    denominator = jnp.einsum("thd,hd->th", queries, key_total, precision=lax.Precision.HIGHEST)
    result = numerator / (denominator[:, :, None] + attn_eps) * live_mask[:, None, None]
    return result.reshape(1, grid_rows, grid_cols, inner_width).astype(jnp.bfloat16)


def solution(mesh):
    in_specs = (
        P("img", "seq", None, None),
        P(),
        P("img", None),
        P(),
        P("img"),
        P("img"),
        P("img", "seq"),
    )
    out_specs = P("img", "seq", None, None)
    plane = mesh.shape["img"] == 4 and mesh.shape["seq"] == 8
    run = functools.partial(fast_body, mesh) if plane else body
    return jax.shard_map(run, mesh=mesh, in_specs=in_specs, out_specs=out_specs, check_vma=False)
```

```python
import functools

import jax
import jax.numpy as jnp
from jax import lax
from jax.experimental import pallas as pl
from jax.experimental.pallas import tpu as pltpu
from jax.sharding import PartitionSpec as P

HDIM = 32
LANES = 128
PARTS = 2

norm_eps = 1e-06
attn_eps = 1e-06


def gray(r):
    return r + r // 2 - 2 * (r // 3)


def half_rows(width):
    return -(-width // 32) * 16


def product(a, b, dims):
    a_high, b_high = a.astype(jnp.bfloat16), b.astype(jnp.bfloat16)
    a_low = (a - a_high.astype(jnp.float32)).astype(jnp.bfloat16)
    b_low = (b - b_high.astype(jnp.float32)).astype(jnp.bfloat16)
    rows = a.shape[0]
    first = lax.dot_general(
        jnp.concatenate([a_high, a_low], axis=0), b_high, dims, preferred_element_type=jnp.float32
    )
    return (
        first[0:rows] + first[rows:]
        + lax.dot_general(a_high, b_low, dims, preferred_element_type=jnp.float32)
    )


def kernel(
    dims,
    tokens_ref, vectors_ref, keep_ref, rows_ref, w_ref,
    out_ref,
    own, wbuf, hid, ends_upper, ends_lower, spread, full, state, pieces, total,
    send_sems, z_sems, left_sems, right_sems, far_sems, twin_sems, piece_sems, total_sems, local_sem,
):
    n_img, n_seq, grid_rows, grid_cols, depth, width, inner = dims
    main_tiles = depth // LANES
    main = main_tiles * LANES
    tail = depth - main
    top = half_rows(width)
    packed = own.shape[0]
    part_rows = packed // PARTS
    n_z = n_seq // 2
    token_count = grid_rows * grid_cols

    seq = lax.axis_index("seq")
    img = lax.axis_index("img")
    core = lax.rem(seq, 2)
    z = seq // 2
    ring = gray(img)
    right = gray(lax.rem(ring + 1, 4))
    left = gray(lax.rem(ring + 3, 4))
    far = gray(lax.rem(ring + 2, 4))
    twin = seq + 1 - 2 * core
    zs = [z, z + 1 - 2 * lax.rem(z, 2), lax.rem(z + 2, 4), 3 - z]
    mine = [2 * q + core for q in zs]
    twins = [2 * q + 1 - core for q in zs]

    barrier = pltpu.get_barrier_semaphore()
    peers = [(img, lax.rem(seq + d, n_seq)) for d in range(1, n_seq)] + [(left, seq), (right, seq)]
    for i, s in peers:
        pl.semaphore_signal(
            barrier, inc=1, device_id={"img": i, "seq": s}, device_id_type=pl.DeviceIdType.MESH
        )

    for j in range(main_tiles):
        own[width * j : width * (j + 1), :] = w_ref[:, LANES * j : LANES * (j + 1)]
    rows_at = lax.broadcasted_iota(jnp.int32, (tail, LANES), 0)
    cols_at = lax.broadcasted_iota(jnp.int32, (tail, LANES), 1)
    base = width * main_tiles
    upper = jnp.dot(
        w_ref[0:top, main:depth], (rows_at == cols_at).astype(jnp.bfloat16),
        preferred_element_type=jnp.float32,
    )
    lower = jnp.dot(
        w_ref[top:width, main:depth], (rows_at + LANES // 2 == cols_at).astype(jnp.bfloat16),
        preferred_element_type=jnp.float32,
    )
    own[base : base + width - top, :] = (upper[0 : width - top] + lower).astype(jnp.bfloat16)
    if 2 * top > width:
        own[base + width - top : base + top, :] = upper[width - top : top].astype(jnp.bfloat16)

    pl.semaphore_wait(barrier, len(peers))

    sends = []

    def part(p):
        return pl.ds(p * part_rows, part_rows)

    def send(src, i, s, p, recv_sem, to_img, to_seq):
        copy = pltpu.make_async_remote_copy(
            src_ref=src,
            dst_ref=wbuf.at[i, s, part(p)],
            send_sem=send_sems.at[len(sends)],
            recv_sem=recv_sem,
            device_id={"img": to_img, "seq": to_seq},
            device_id_type=pl.DeviceIdType.MESH,
        )
        copy.start()
        sends.append(copy)

    def arrive(i, s, p, recv_sem):
        block = wbuf.at[i, s, part(p)]
        pltpu.make_async_remote_copy(
            src_ref=block, dst_ref=block, send_sem=send_sems.at[0], recv_sem=recv_sem,
            device_id={"img": img, "seq": twin}, device_id_type=pl.DeviceIdType.MESH,
        ).wait_recv()
        return block

    keep_own = pltpu.make_async_copy(own, wbuf.at[img, seq], local_sem)
    keep_own.start()
    for p in range(PARTS):
        src = own.at[part(p)]
        send(src, img, seq, p, left_sems.at[0, p], right, seq)
        send(src, img, seq, p, right_sems.at[0, p], left, seq)
        send(src, img, seq, p, z_sems.at[0, p], img, mine[1])
        send(src, img, seq, p, twin_sems.at[0, 0, p], img, twin)
    for k in range(2, n_z):
        for p in range(PARTS):
            send(own.at[part(p)], img, seq, p, z_sems.at[k - 1, p], img, mine[k])

    flag = jnp.full((1, depth * n_img), keep_ref[0])
    condition = jnp.where(flag > 0, vectors_ref[1:2, :].astype(jnp.float32), vectors_ref[2:3, :].astype(jnp.float32))
    pair = jnp.concatenate([vectors_ref[0:1, :].astype(jnp.float32), condition], axis=0).astype(jnp.bfloat16)
    row_is = lax.broadcasted_iota(jnp.int32, (2, 2 * LANES), 0)
    col_is = lax.broadcasted_iota(jnp.int32, (2, 2 * LANES), 1) // LANES
    spread[...] = lax.dot_general(
        pair, (row_is == col_is).astype(jnp.bfloat16), (((0,), (0,)), ((), ())),
        preferred_element_type=jnp.float32,
    )
    ends_upper[...] = jnp.zeros_like(ends_upper)
    ends_lower[...] = jnp.zeros_like(ends_lower)
    for t in range(grid_rows):
        cols = slice(grid_cols * t, grid_cols * (t + 1))
        features = tokens_ref[t].astype(jnp.float32)
        mean_square = jnp.mean(features * features, axis=0, keepdims=True)
        scale = lax.rsqrt(mean_square + norm_eps)
        for i in range(n_img):
            rows = slice(depth * i, depth * (i + 1))
            hidden = (
                tokens_ref[t, rows, :].astype(jnp.float32) * scale * spread[rows, 0:LANES]
                + spread[rows, LANES:]
            ).astype(jnp.bfloat16)
            hid[main * i : main * (i + 1), cols] = hidden[0:main]
            ends_upper[LANES * i : LANES * i + tail, cols] = hidden[main:depth]
            half = LANES * i + LANES // 2
            ends_lower[half : half + tail, cols] = hidden[main:depth]

    keep_own.wait()

    def project(s):
        block = jnp.concatenate(
            [wbuf[i, s, width * j : width * (j + 1), :] for i in range(n_img) for j in range(main_tiles)],
            axis=1,
        )
        ends = jnp.concatenate([wbuf[i, s, base : base + top, :] for i in range(n_img)], axis=1)
        acc = jnp.dot(block, hid[...], preferred_element_type=jnp.float32)
        acc_upper = jnp.dot(ends, ends_upper[...], preferred_element_type=jnp.float32)
        acc_lower = jnp.dot(ends[0 : width - top], ends_lower[...], preferred_element_type=jnp.float32)
        at = pl.multiple_of(s * width, width)
        full[pl.ds(at, top), :] = acc[0:top] + acc_upper
        full[pl.ds(at + top, width - top), :] = acc[top:width] + acc_lower

    def finish(k):
        for p in range(PARTS):
            for at, i in enumerate((img, left, right)):
                arrive(i, twins[k], p, twin_sems.at[k, at, p])
        arrive(far, twins[k], 0, twin_sems.at[k, 3, 0])
        arrive(far, twins[k], 1, twin_sems.at[k, 3, 1])
        project(mine[k])
        project(twins[k])

    for k in range(n_z):
        if k + 1 < n_z:
            s = mine[k + 1]
            for p in range(PARTS):
                src = arrive(img, s, p, z_sems.at[k, p])
                send(src, img, s, p, left_sems.at[k + 1, p], right, seq)
                send(src, img, s, p, right_sems.at[k + 1, p], left, seq)
                send(src, img, s, p, twin_sems.at[k + 1, 0, p], img, twin)
        s = mine[k]
        for p in range(PARTS):
            src = arrive(left, s, p, left_sems.at[k, p])
            if p == 0:
                send(src, left, s, p, far_sems.at[k, 0], right, seq)
            send(src, left, s, p, twin_sems.at[k, 1, p], img, twin)
            src = arrive(right, s, p, right_sems.at[k, p])
            if p == 1:
                send(src, right, s, p, far_sems.at[k, 1], left, seq)
            send(src, right, s, p, twin_sems.at[k, 2, p], img, twin)
        if k > 0:
            finish(k - 1)
        for p in range(PARTS):
            src = arrive(far, s, p, far_sems.at[k, p])
            send(src, far, s, p, twin_sems.at[k, 3, p], img, twin)
    finish(n_z - 1)

    groups = inner // LANES
    head_of_row = lax.broadcasted_iota(jnp.int32, (LANES, LANES), 0) // HDIM
    head_of_col = lax.broadcasted_iota(jnp.int32, (LANES, LANES), 1) // HDIM
    same = (head_of_row == head_of_col).astype(jnp.float32)
    live_rows = seq * grid_rows + lax.broadcasted_iota(jnp.int32, (1, token_count), 1) // grid_cols
    live = (live_rows < rows_ref[0]).astype(jnp.float32)
    state[...] = jnp.zeros_like(state)
    by_lanes = (((1,), (1,)), ((), ()))
    by_rows = (((1,), (0,)), ((), ()))
    ones = jnp.ones((8, token_count), jnp.float32)
    for g in range(groups):
        keys = jax.nn.relu(full[inner + LANES * g : inner + LANES * (g + 1), :]) * live
        values = full[2 * inner + LANES * g : 2 * inner + LANES * (g + 1), :]
        outer = product(jnp.concatenate([values, ones], axis=0), keys, by_lanes)
        kept = outer[0:LANES] * same
        state[HDIM * g : HDIM * (g + 1), :] = kept[0:32] + kept[32:64] + kept[64:96] + kept[96:128]
        state[HDIM * groups + g : HDIM * groups + g + 1, :] = outer[LANES : LANES + 1]

    piece = state.shape[0] // n_seq

    def piece_of(ref, s):
        return ref.at[pl.ds(pl.multiple_of(s * piece, piece), piece)]

    scattered, gathered = [], []
    for d in range(1, n_seq):
        to = lax.rem(seq + d, n_seq)
        copy = pltpu.make_async_remote_copy(
            src_ref=piece_of(state, to), dst_ref=pieces.at[d - 1],
            send_sem=send_sems.at[len(sends) + d - 1], recv_sem=piece_sems.at[d - 1],
            device_id={"img": img, "seq": to}, device_id_type=pl.DeviceIdType.MESH,
        )
        copy.start()
        scattered.append(copy)
    summed = state[pl.ds(pl.multiple_of(seq * piece, piece), piece), :]
    for d in range(1, n_seq):
        scattered[d - 1].wait_recv()
        summed = summed + pieces[d - 1]
    total[pl.ds(pl.multiple_of(seq * piece, piece), piece), :] = summed
    for d in range(1, n_seq):
        copy = pltpu.make_async_remote_copy(
            src_ref=piece_of(total, seq), dst_ref=piece_of(total, seq),
            send_sem=send_sems.at[len(sends) + n_seq - 1 + d - 1], recv_sem=total_sems.at[d - 1],
            device_id={"img": img, "seq": lax.rem(seq + d, n_seq)}, device_id_type=pl.DeviceIdType.MESH,
        )
        copy.start()
        gathered.append(copy)
    for d in range(1, n_seq):
        block = piece_of(total, lax.rem(seq + n_seq - d, n_seq))
        pltpu.make_async_remote_copy(
            src_ref=block, dst_ref=block, send_sem=send_sems.at[0], recv_sem=total_sems.at[d - 1],
            device_id={"img": img, "seq": twin}, device_id_type=pl.DeviceIdType.MESH,
        ).wait_recv()

    for g in range(groups):
        queries = jax.nn.relu(full[LANES * g : LANES * (g + 1), :])
        compact = total[HDIM * g : HDIM * (g + 1), :]
        outer = jnp.concatenate([compact] * (LANES // HDIM), axis=0) * same
        key_total = total[HDIM * groups + g : HDIM * groups + g + 1, :] * same
        both = product(jnp.concatenate([outer, key_total], axis=0), queries, by_rows)
        result = (both[0:LANES] / (both[LANES:] + attn_eps) * live).astype(out_ref.dtype)
        for t in range(grid_rows):
            out_ref[t, LANES * g : LANES * (g + 1), :] = result[:, grid_cols * t : grid_cols * (t + 1)]

    for copy in sends + scattered + gathered:
        copy.wait_send()


def fast_body(mesh, tokens, norm_gain, caption, null_caption, keep, bucket_rows, w_qkv):
    n_img, n_seq = mesh.shape["img"], mesh.shape["seq"]
    _, grid_rows, grid_cols, features = tokens.shape
    depth, width = w_qkv.shape
    inner = width * n_seq // 3
    token_count = grid_rows * grid_cols
    n_z = n_seq // 2
    packed = width * (depth // LANES) + half_rows(width)
    state_rows = (HDIM + 1) * (inner // LANES)
    piece = -(-state_rows // (8 * n_seq)) * 8
    dims = (n_img, n_seq, grid_rows, grid_cols, depth, width, inner)
    vmem = pl.BlockSpec(memory_space=pltpu.VMEM)
    smem = pl.BlockSpec(memory_space=pltpu.SMEM)
    dma = pltpu.SemaphoreType.DMA
    out = pl.pallas_call(
        functools.partial(kernel, dims),
        out_shape=jax.ShapeDtypeStruct((grid_rows, inner, grid_cols), jnp.bfloat16),
        in_specs=[vmem, vmem, smem, smem, vmem],
        out_specs=vmem,
        scratch_shapes=[
            pltpu.VMEM((packed, LANES), jnp.bfloat16),
            pltpu.VMEM((n_img, n_seq, packed, LANES), jnp.bfloat16),
            pltpu.VMEM((n_img * (depth // LANES) * LANES, token_count), jnp.bfloat16),
            pltpu.VMEM((n_img * LANES, token_count), jnp.bfloat16),
            pltpu.VMEM((n_img * LANES, token_count), jnp.bfloat16),
            pltpu.VMEM((features, 2 * LANES), jnp.float32),
            pltpu.VMEM((3 * inner, token_count), jnp.float32),
            pltpu.VMEM((piece * n_seq, LANES), jnp.float32),
            pltpu.VMEM((n_seq - 1, piece, LANES), jnp.float32),
            pltpu.VMEM((piece * n_seq, LANES), jnp.float32),
            dma((96,)),
            dma((n_z - 1, PARTS)),
            dma((n_z, PARTS)),
            dma((n_z, PARTS)),
            dma((n_z, PARTS)),
            dma((n_z, 4, PARTS)),
            dma((n_seq - 1,)),
            dma((n_seq - 1,)),
            dma(()),
        ],
        compiler_params=pltpu.CompilerParams(
            collective_id=0, has_side_effects=True, vmem_limit_bytes=56 * 1024 * 1024
        ),
        cost_estimate=pl.CostEstimate(
            flops=2 * token_count * features * 3 * inner, bytes_accessed=4 * token_count * features,
            transcendentals=0,
        ),
    )(
        tokens.transpose(0, 1, 3, 2).reshape(grid_rows, features, grid_cols),
        jnp.stack([norm_gain, caption[0], null_caption]), keep, bucket_rows, w_qkv.T,
    )
    return out.transpose(0, 2, 1).reshape(1, grid_rows, grid_cols, inner)


def body(tokens, norm_gain, caption, null_caption, keep, bucket_rows, w_qkv):
    grid_rows = tokens.shape[1]
    grid_cols = tokens.shape[2]
    features_count = tokens.shape[3]
    token_count = grid_rows * grid_cols
    features = tokens.reshape(token_count, features_count).astype(jnp.float32)
    mean_square = jnp.mean(features * features, axis=1, keepdims=True)
    condition = jnp.where(keep[0] > 0, caption[0], null_caption).astype(jnp.float32)
    hidden = (
        features * lax.rsqrt(mean_square + norm_eps) * norm_gain.astype(jnp.float32) + condition
    ).astype(jnp.bfloat16)
    rows_whole = lax.all_gather(w_qkv, "img", axis=0, tiled=True)
    projected = jnp.dot(
        hidden,
        lax.all_gather(rows_whole, "seq", axis=1, tiled=True),
        preferred_element_type=jnp.float32,
    )
    inner_width = projected.shape[1] // 3
    head_count = inner_width // HDIM
    grid_row = (
        lax.axis_index("seq") * grid_rows + jnp.arange(token_count, dtype=jnp.int32) // grid_cols
    )
    live_mask = (grid_row < bucket_rows[0]).astype(jnp.float32)
    queries = jax.nn.relu(projected[:, :inner_width]).reshape(token_count, head_count, HDIM)
    keys_relu = jax.nn.relu(projected[:, inner_width : 2 * inner_width]).reshape(
        token_count, head_count, HDIM
    )
    keys_relu = keys_relu * live_mask[:, None, None]
    values = projected[:, 2 * inner_width :].reshape(token_count, head_count, HDIM)
    state_outer = jnp.einsum("thd,the->hde", keys_relu, values, precision=lax.Precision.HIGHEST)
    key_total = jnp.sum(keys_relu, axis=0)
    state_outer, key_total = lax.psum((state_outer, key_total), "seq")
    numerator = jnp.einsum("thd,hde->the", queries, state_outer, precision=lax.Precision.HIGHEST)
    denominator = jnp.einsum("thd,hd->th", queries, key_total, precision=lax.Precision.HIGHEST)
    result = numerator / (denominator[:, :, None] + attn_eps) * live_mask[:, None, None]
    return result.reshape(1, grid_rows, grid_cols, inner_width).astype(jnp.bfloat16)


def solution(mesh):
    in_specs = (
        P("img", "seq", None, None),
        P(),
        P("img", None),
        P(),
        P("img"),
        P("img"),
        P("img", "seq"),
    )
    out_specs = P("img", "seq", None, None)
    plane = mesh.shape["img"] == 4 and mesh.shape["seq"] == 8
    run = functools.partial(fast_body, mesh) if plane else body
    return jax.shard_map(run, mesh=mesh, in_specs=in_specs, out_specs=out_specs, check_vma=False)
```

```python
import functools

import jax
import jax.numpy as jnp
from jax import lax
from jax.experimental import pallas as pl
from jax.experimental.pallas import tpu as pltpu
from jax.sharding import PartitionSpec as P

HDIM = 32
LANES = 128

norm_eps = 1e-06
attn_eps = 1e-06


def gray(r):
    return r + r // 2 - 2 * (r // 3)


def half_rows(width):
    return -(-width // 32) * 16


def parts_of(packed):
    units = packed // 16
    b = round(units * 2 / 9)
    a = units - b
    cuts = [0, (a + 1) // 2, a, a + (b + 1) // 2, units]
    cuts = [16 * c for c in cuts]

    def span(i, j):
        return (cuts[i], cuts[j] - cuts[i])

    return span(0, 2), span(0, 1), span(1, 2), span(2, 4), span(2, 3), span(3, 4)


def product(a, b, dims):
    a_high, b_high = a.astype(jnp.bfloat16), b.astype(jnp.bfloat16)
    a_low = (a - a_high.astype(jnp.float32)).astype(jnp.bfloat16)
    b_low = (b - b_high.astype(jnp.float32)).astype(jnp.bfloat16)
    rows = a.shape[0]
    first = lax.dot_general(
        jnp.concatenate([a_high, a_low], axis=0), b_high, dims, preferred_element_type=jnp.float32
    )
    return (
        first[0:rows] + first[rows:]
        + lax.dot_general(a_high, b_low, dims, preferred_element_type=jnp.float32)
    )


def kernel(
    dims,
    tokens_ref, vectors_ref, keep_ref, rows_ref, w_ref,
    out_ref,
    own, wbuf, hid, ends_upper, ends_lower, spread, full, state, pieces, total,
    send_sems, in_sems, twin_sems, piece_sems, total_sems, local_sem,
):
    n_img, n_seq, grid_rows, grid_cols, depth, width, inner = dims
    main_tiles = depth // LANES
    main = main_tiles * LANES
    tail = depth - main
    top = half_rows(width)
    packed = own.shape[0]
    A, A0, A1, B, B0, B1 = parts_of(packed)
    n_z = n_seq // 2
    token_count = grid_rows * grid_cols

    seq = lax.axis_index("seq")
    img = lax.axis_index("img")
    core = lax.rem(seq, 2)
    z = seq // 2
    ring = gray(img)
    right = gray(lax.rem(ring + 1, 4))
    left = gray(lax.rem(ring + 3, 4))
    far = gray(lax.rem(ring + 2, 4))
    twin = seq + 1 - 2 * core
    zs = [z, z + 1 - 2 * lax.rem(z, 2), 2 - z // 2, 3 - 3 * (z // 2)]
    mine = [2 * q + core for q in zs]
    twins = [2 * q + 1 - core for q in zs]

    barrier = pltpu.get_barrier_semaphore()
    peers = [(img, lax.rem(seq + d, n_seq)) for d in range(1, n_seq)] + [(left, seq), (right, seq)]
    for i, s in peers:
        pl.semaphore_signal(
            barrier, inc=1, device_id={"img": i, "seq": s}, device_id_type=pl.DeviceIdType.MESH
        )

    for j in range(main_tiles):
        own[width * j : width * (j + 1), :] = w_ref[:, LANES * j : LANES * (j + 1)]
    rows_at = lax.broadcasted_iota(jnp.int32, (tail, LANES), 0)
    cols_at = lax.broadcasted_iota(jnp.int32, (tail, LANES), 1)
    base = width * main_tiles
    upper = jnp.dot(
        w_ref[0:top, main:depth], (rows_at == cols_at).astype(jnp.bfloat16),
        preferred_element_type=jnp.float32,
    )
    lower = jnp.dot(
        w_ref[top:width, main:depth], (rows_at + LANES // 2 == cols_at).astype(jnp.bfloat16),
        preferred_element_type=jnp.float32,
    )
    own[base : base + width - top, :] = (upper[0 : width - top] + lower).astype(jnp.bfloat16)
    if 2 * top > width:
        own[base + width - top : base + top, :] = upper[width - top : top].astype(jnp.bfloat16)

    pl.semaphore_wait(barrier, len(peers))

    sends = []

    def send(src, i, s, span, recv_sem, to_img, to_seq, when=None):
        copy = pltpu.make_async_remote_copy(
            src_ref=src.at[pl.ds(*span)],
            dst_ref=wbuf.at[i, s, pl.ds(*span)],
            send_sem=send_sems.at[len(sends)],
            recv_sem=recv_sem,
            device_id={"img": to_img, "seq": to_seq},
            device_id_type=pl.DeviceIdType.MESH,
        )
        if when is None:
            copy.start()
        else:
            pl.when(when)(copy.start)
        sends.append((copy, when))

    def arrive(i, s, span, recv_sem):
        block = wbuf.at[i, s, pl.ds(*span)]
        pltpu.make_async_remote_copy(
            src_ref=block, dst_ref=block, send_sem=send_sems.at[0], recv_sem=recv_sem,
            device_id={"img": img, "seq": twin}, device_id_type=pl.DeviceIdType.MESH,
        ).wait_recv()

    slot = {A0: 0, A1: 1, B0: 2, B1: 3, B: 2}

    def get(i, q, *spans):
        for span in spans:
            arrive(i, 2 * q + core, span, in_sems.at[i, q, slot[span]])

    def give(src, i, q, to, *spans):
        for span in spans:
            send(src, i, 2 * q + core, span, in_sems.at[i, q, slot[span]], to, seq)

    def share(src, i, q, *spans):
        for span in spans:
            send(src, i, 2 * q + core, span, twin_sems.at[i, q, 0 if span == A else 1], img, twin)

    def start_line(src, i, spans):
        for span in spans:
            sem = in_sems.at[i, z, slot[span]]
            send(src, i, seq, span, sem, img, lax.rem(seq + 2, n_seq), z < n_z - 1)
            send(src, i, seq, span, sem, img, lax.rem(seq + n_seq - 2, n_seq), z > 0)

    def relay(src, i, q, spans):
        to = z - 1 + 2 * (q < z).astype(jnp.int32)
        inside = jnp.logical_and(to >= 0, to < n_z)
        to_seq = lax.rem(2 * to + core + n_seq, n_seq)
        for span in spans:
            send(src, i, 2 * q + core, span, in_sems.at[i, q, slot[span]], img, to_seq, inside)

    def block_of(i, q):
        return wbuf.at[i, 2 * q + core]

    keep_own = pltpu.make_async_copy(own, wbuf.at[img, seq], local_sem)
    keep_own.start()
    for span in (A0, A1):
        give(own, img, z, right, span)
        give(own, img, z, left, span)
        start_line(own, img, [span])
    for span in (B0, B1):
        give(own, img, z, right, span)
        give(own, img, z, left, span)
    start_line(own, img, [B])
    share(own, img, z, A, B)

    flag = jnp.full((1, depth * n_img), keep_ref[0])
    condition = jnp.where(flag > 0, vectors_ref[1:2, :].astype(jnp.float32), vectors_ref[2:3, :].astype(jnp.float32))
    pair = jnp.concatenate([vectors_ref[0:1, :].astype(jnp.float32), condition], axis=0).astype(jnp.bfloat16)
    row_is = lax.broadcasted_iota(jnp.int32, (2, 2 * LANES), 0)
    col_is = lax.broadcasted_iota(jnp.int32, (2, 2 * LANES), 1) // LANES
    spread[...] = lax.dot_general(
        pair, (row_is == col_is).astype(jnp.bfloat16), (((0,), (0,)), ((), ())),
        preferred_element_type=jnp.float32,
    )
    ends_upper[...] = jnp.zeros_like(ends_upper)
    ends_lower[...] = jnp.zeros_like(ends_lower)
    for t in range(grid_rows):
        cols = slice(grid_cols * t, grid_cols * (t + 1))
        features = tokens_ref[t].astype(jnp.float32)
        mean_square = jnp.mean(features * features, axis=0, keepdims=True)
        scale = lax.rsqrt(mean_square + norm_eps)
        for i in range(n_img):
            rows = slice(depth * i, depth * (i + 1))
            hidden = (
                tokens_ref[t, rows, :].astype(jnp.float32) * scale * spread[rows, 0:LANES]
                + spread[rows, LANES:]
            ).astype(jnp.bfloat16)
            hid[main * i : main * (i + 1), cols] = hidden[0:main]
            ends_upper[LANES * i : LANES * i + tail, cols] = hidden[main:depth]
            half = LANES * i + LANES // 2
            ends_lower[half : half + tail, cols] = hidden[main:depth]

    keep_own.wait()

    def project(s):
        block = jnp.concatenate(
            [wbuf[i, s, width * j : width * (j + 1), :] for i in range(n_img) for j in range(main_tiles)],
            axis=1,
        )
        ends = jnp.concatenate([wbuf[i, s, base : base + top, :] for i in range(n_img)], axis=1)
        acc = jnp.dot(block, hid[...], preferred_element_type=jnp.float32)
        acc_upper = jnp.dot(ends, ends_upper[...], preferred_element_type=jnp.float32)
        acc_lower = jnp.dot(ends[0 : width - top], ends_lower[...], preferred_element_type=jnp.float32)
        at = pl.multiple_of(s * width, width)
        full[pl.ds(at, top), :] = acc[0:top] + acc_upper
        full[pl.ds(at + top, width - top), :] = acc[top:width] + acc_lower

    def finish(k):
        for i in (img, left, right, far):
            arrive(i, twins[k], A, twin_sems.at[i, zs[k], 0])
            arrive(i, twins[k], B, twin_sems.at[i, zs[k], 1])
        project(mine[k])
        project(twins[k])

    def side_rows(q):
        for i in (left, right, far):
            get(i, q, B)
            relay(block_of(i, q), i, q, [B])
            share(block_of(i, q), i, q, B)

    for k in range(n_z):
        if k + 1 < n_z:
            q = zs[k + 1]
            src = block_of(img, q)
            for span in (A0, A1):
                get(img, q, span)
                give(src, img, q, right, span)
                give(src, img, q, left, span)
                relay(src, img, q, [span])
            get(img, q, B)
            relay(src, img, q, [B])
            share(src, img, q, A, B)
        q = zs[k]
        from_left, from_right, from_far = block_of(left, q), block_of(right, q), block_of(far, q)
        get(left, q, A0)
        give(from_left, left, q, right, A0)
        get(right, q, A0, A1)
        give(from_right, right, q, left, A1)
        share(from_right, right, q, A)
        get(left, q, A1)
        share(from_left, left, q, A)
        if k == 0:
            get(left, q, B0)
            give(from_left, left, q, right, B0)
            get(right, q, B0, B1)
            give(from_right, right, q, left, B1)
            start_line(from_right, right, [B])
            share(from_right, right, q, B)
            get(left, q, B1)
            start_line(from_left, left, [B])
            share(from_left, left, q, B)
        elif k == 1:
            side_rows(q)
        elif k == 2:
            side_rows(q)
            side_rows(zs[3])
        get(far, q, A0, A1)
        share(from_far, far, q, A)
        if k == 0:
            get(far, q, B0, B1)
            start_line(from_far, far, [B])
            share(from_far, far, q, B)
        else:
            finish(k - 1)
    finish(n_z - 1)

    groups = inner // LANES
    head_of_row = lax.broadcasted_iota(jnp.int32, (LANES, LANES), 0) // HDIM
    head_of_col = lax.broadcasted_iota(jnp.int32, (LANES, LANES), 1) // HDIM
    same = (head_of_row == head_of_col).astype(jnp.float32)
    live_rows = seq * grid_rows + lax.broadcasted_iota(jnp.int32, (1, token_count), 1) // grid_cols
    live = (live_rows < rows_ref[0]).astype(jnp.float32)
    state[...] = jnp.zeros_like(state)
    by_lanes = (((1,), (1,)), ((), ()))
    by_rows = (((1,), (0,)), ((), ()))
    ones = jnp.ones((8, token_count), jnp.float32)
    for g in range(groups):
        keys = jax.nn.relu(full[inner + LANES * g : inner + LANES * (g + 1), :]) * live
        values = full[2 * inner + LANES * g : 2 * inner + LANES * (g + 1), :]
        outer = product(jnp.concatenate([values, ones], axis=0), keys, by_lanes)
        kept = outer[0:LANES] * same
        state[HDIM * g : HDIM * (g + 1), :] = kept[0:32] + kept[32:64] + kept[64:96] + kept[96:128]
        state[HDIM * groups + g : HDIM * groups + g + 1, :] = outer[LANES : LANES + 1]

    piece = state.shape[0] // n_seq

    def piece_of(ref, s):
        return ref.at[pl.ds(pl.multiple_of(s * piece, piece), piece)]

    scattered, gathered = [], []
    for d in range(1, n_seq):
        to = lax.rem(seq + d, n_seq)
        copy = pltpu.make_async_remote_copy(
            src_ref=piece_of(state, to), dst_ref=pieces.at[d - 1],
            send_sem=send_sems.at[len(sends) + d - 1], recv_sem=piece_sems.at[d - 1],
            device_id={"img": img, "seq": to}, device_id_type=pl.DeviceIdType.MESH,
        )
        copy.start()
        scattered.append(copy)
    summed = state[pl.ds(pl.multiple_of(seq * piece, piece), piece), :]
    for d in range(1, n_seq):
        scattered[d - 1].wait_recv()
        summed = summed + pieces[d - 1]
    total[pl.ds(pl.multiple_of(seq * piece, piece), piece), :] = summed
    for d in range(1, n_seq):
        copy = pltpu.make_async_remote_copy(
            src_ref=piece_of(total, seq), dst_ref=piece_of(total, seq),
            send_sem=send_sems.at[len(sends) + n_seq - 1 + d - 1], recv_sem=total_sems.at[d - 1],
            device_id={"img": img, "seq": lax.rem(seq + d, n_seq)}, device_id_type=pl.DeviceIdType.MESH,
        )
        copy.start()
        gathered.append(copy)
    for d in range(1, n_seq):
        block = piece_of(total, lax.rem(seq + n_seq - d, n_seq))
        pltpu.make_async_remote_copy(
            src_ref=block, dst_ref=block, send_sem=send_sems.at[0], recv_sem=total_sems.at[d - 1],
            device_id={"img": img, "seq": twin}, device_id_type=pl.DeviceIdType.MESH,
        ).wait_recv()

    for g in range(groups):
        queries = jax.nn.relu(full[LANES * g : LANES * (g + 1), :])
        compact = total[HDIM * g : HDIM * (g + 1), :]
        outer = jnp.concatenate([compact] * (LANES // HDIM), axis=0) * same
        key_total = total[HDIM * groups + g : HDIM * groups + g + 1, :] * same
        both = product(jnp.concatenate([outer, key_total], axis=0), queries, by_rows)
        result = (both[0:LANES] / (both[LANES:] + attn_eps) * live).astype(out_ref.dtype)
        for t in range(grid_rows):
            out_ref[t, LANES * g : LANES * (g + 1), :] = result[:, grid_cols * t : grid_cols * (t + 1)]

    for copy, when in sends:
        if when is None:
            copy.wait_send()
        else:
            pl.when(when)(copy.wait_send)
    for copy in scattered + gathered:
        copy.wait_send()


def fast_body(mesh, tokens, norm_gain, caption, null_caption, keep, bucket_rows, w_qkv):
    n_img, n_seq = mesh.shape["img"], mesh.shape["seq"]
    _, grid_rows, grid_cols, features = tokens.shape
    depth, width = w_qkv.shape
    inner = width * n_seq // 3
    token_count = grid_rows * grid_cols
    n_z = n_seq // 2
    packed = width * (depth // LANES) + half_rows(width)
    state_rows = (HDIM + 1) * (inner // LANES)
    piece = -(-state_rows // (8 * n_seq)) * 8
    dims = (n_img, n_seq, grid_rows, grid_cols, depth, width, inner)
    vmem = pl.BlockSpec(memory_space=pltpu.VMEM)
    smem = pl.BlockSpec(memory_space=pltpu.SMEM)
    dma = pltpu.SemaphoreType.DMA
    out = pl.pallas_call(
        functools.partial(kernel, dims),
        out_shape=jax.ShapeDtypeStruct((grid_rows, inner, grid_cols), jnp.bfloat16),
        in_specs=[vmem, vmem, smem, smem, vmem],
        out_specs=vmem,
        scratch_shapes=[
            pltpu.VMEM((packed, LANES), jnp.bfloat16),
            pltpu.VMEM((n_img, n_seq, packed, LANES), jnp.bfloat16),
            pltpu.VMEM((n_img * (depth // LANES) * LANES, token_count), jnp.bfloat16),
            pltpu.VMEM((n_img * LANES, token_count), jnp.bfloat16),
            pltpu.VMEM((n_img * LANES, token_count), jnp.bfloat16),
            pltpu.VMEM((features, 2 * LANES), jnp.float32),
            pltpu.VMEM((3 * inner, token_count), jnp.float32),
            pltpu.VMEM((piece * n_seq, LANES), jnp.float32),
            pltpu.VMEM((n_seq - 1, piece, LANES), jnp.float32),
            pltpu.VMEM((piece * n_seq, LANES), jnp.float32),
            dma((192,)),
            dma((n_img, n_z, 4)),
            dma((n_img, n_z, 2)),
            dma((n_seq - 1,)),
            dma((n_seq - 1,)),
            dma(()),
        ],
        compiler_params=pltpu.CompilerParams(
            collective_id=0, has_side_effects=True, vmem_limit_bytes=56 * 1024 * 1024
        ),
        cost_estimate=pl.CostEstimate(
            flops=2 * token_count * features * 3 * inner, bytes_accessed=4 * token_count * features,
            transcendentals=0,
        ),
    )(
        tokens.transpose(0, 1, 3, 2).reshape(grid_rows, features, grid_cols),
        jnp.stack([norm_gain, caption[0], null_caption]), keep, bucket_rows, w_qkv.T,
    )
    return out.transpose(0, 2, 1).reshape(1, grid_rows, grid_cols, inner)


def body(tokens, norm_gain, caption, null_caption, keep, bucket_rows, w_qkv):
    grid_rows = tokens.shape[1]
    grid_cols = tokens.shape[2]
    features_count = tokens.shape[3]
    token_count = grid_rows * grid_cols
    features = tokens.reshape(token_count, features_count).astype(jnp.float32)
    mean_square = jnp.mean(features * features, axis=1, keepdims=True)
    condition = jnp.where(keep[0] > 0, caption[0], null_caption).astype(jnp.float32)
    hidden = (
        features * lax.rsqrt(mean_square + norm_eps) * norm_gain.astype(jnp.float32) + condition
    ).astype(jnp.bfloat16)
    rows_whole = lax.all_gather(w_qkv, "img", axis=0, tiled=True)
    projected = jnp.dot(
        hidden,
        lax.all_gather(rows_whole, "seq", axis=1, tiled=True),
        preferred_element_type=jnp.float32,
    )
    inner_width = projected.shape[1] // 3
    head_count = inner_width // HDIM
    grid_row = (
        lax.axis_index("seq") * grid_rows + jnp.arange(token_count, dtype=jnp.int32) // grid_cols
    )
    live_mask = (grid_row < bucket_rows[0]).astype(jnp.float32)
    queries = jax.nn.relu(projected[:, :inner_width]).reshape(token_count, head_count, HDIM)
    keys_relu = jax.nn.relu(projected[:, inner_width : 2 * inner_width]).reshape(
        token_count, head_count, HDIM
    )
    keys_relu = keys_relu * live_mask[:, None, None]
    values = projected[:, 2 * inner_width :].reshape(token_count, head_count, HDIM)
    state_outer = jnp.einsum("thd,the->hde", keys_relu, values, precision=lax.Precision.HIGHEST)
    key_total = jnp.sum(keys_relu, axis=0)
    state_outer, key_total = lax.psum((state_outer, key_total), "seq")
    numerator = jnp.einsum("thd,hde->the", queries, state_outer, precision=lax.Precision.HIGHEST)
    denominator = jnp.einsum("thd,hd->th", queries, key_total, precision=lax.Precision.HIGHEST)
    result = numerator / (denominator[:, :, None] + attn_eps) * live_mask[:, None, None]
    return result.reshape(1, grid_rows, grid_cols, inner_width).astype(jnp.bfloat16)


def solution(mesh):
    in_specs = (
        P("img", "seq", None, None),
        P(),
        P("img", None),
        P(),
        P("img"),
        P("img"),
        P("img", "seq"),
    )
    out_specs = P("img", "seq", None, None)
    plane = mesh.shape["img"] == 4 and mesh.shape["seq"] == 8
    run = functools.partial(fast_body, mesh) if plane else body
    return jax.shard_map(run, mesh=mesh, in_specs=in_specs, out_specs=out_specs, check_vma=False)
```

```python
import functools

import jax
import jax.numpy as jnp
from jax import lax
from jax.experimental import pallas as pl
from jax.experimental.pallas import tpu as pltpu
from jax.sharding import PartitionSpec as P

HDIM = 32
LANES = 128

norm_eps = 1e-06
attn_eps = 1e-06


def gray(r):
    return r + r // 2 - 2 * (r // 3)


def half_rows(width):
    return -(-width // 32) * 16


def parts_of(packed):
    units = packed // 16
    b = round(units * 2 / 9)
    a = units - b
    cuts = [0, (a + 1) // 2, a, a + (b + 1) // 2, units]
    cuts = [16 * c for c in cuts]

    def span(i, j):
        return (cuts[i], cuts[j] - cuts[i])

    return span(0, 2), span(0, 1), span(1, 2), span(2, 4), span(2, 3), span(3, 4)


def product(a, b, dims):
    a_high, b_high = a.astype(jnp.bfloat16), b.astype(jnp.bfloat16)
    a_low = (a - a_high.astype(jnp.float32)).astype(jnp.bfloat16)
    b_low = (b - b_high.astype(jnp.float32)).astype(jnp.bfloat16)
    rows = a.shape[0]
    first = lax.dot_general(
        jnp.concatenate([a_high, a_low], axis=0), b_high, dims, preferred_element_type=jnp.float32
    )
    return (
        first[0:rows] + first[rows:]
        + lax.dot_general(a_high, b_low, dims, preferred_element_type=jnp.float32)
    )


def kernel(
    dims,
    tokens_ref, vectors_ref, keep_ref, rows_ref, w_ref,
    out_ref,
    own, wbuf, hid, ends_upper, ends_lower, spread, returns, full, state, pieces, total,
    send_sems, in_sems, swap_send, swap_recv, piece_sems, total_sems, local_sem,
):
    n_img, n_seq, grid_rows, grid_cols, depth, width, inner = dims
    main_tiles = depth // LANES
    main = main_tiles * LANES
    tail = depth - main
    top = half_rows(width)
    packed = own.shape[0]
    A, A0, A1, B, B0, B1 = parts_of(packed)
    n_z = n_seq // 2
    token_count = grid_rows * grid_cols

    seq = lax.axis_index("seq")
    img = lax.axis_index("img")
    core = lax.rem(seq, 2)
    z = seq // 2
    ring = gray(img)
    right = gray(lax.rem(ring + 1, 4))
    left = gray(lax.rem(ring + 3, 4))
    far = gray(lax.rem(ring + 2, 4))
    twin = seq + 1 - 2 * core
    zs = [z, z + 1 - 2 * lax.rem(z, 2), 2 - z // 2, 3 - 3 * (z // 2)]
    mine = [2 * q + core for q in zs]
    twins = [2 * q + 1 - core for q in zs]

    barrier = pltpu.get_barrier_semaphore()
    peers = [(img, lax.rem(seq + d, n_seq)) for d in range(1, n_seq)] + [(left, seq), (right, seq)]
    for i, s in peers:
        pl.semaphore_signal(
            barrier, inc=1, device_id={"img": i, "seq": s}, device_id_type=pl.DeviceIdType.MESH
        )

    for j in range(main_tiles):
        own[width * j : width * (j + 1), :] = w_ref[:, LANES * j : LANES * (j + 1)]
    rows_at = lax.broadcasted_iota(jnp.int32, (tail, LANES), 0)
    cols_at = lax.broadcasted_iota(jnp.int32, (tail, LANES), 1)
    base = width * main_tiles
    upper = jnp.dot(
        w_ref[0:top, main:depth], (rows_at == cols_at).astype(jnp.bfloat16),
        preferred_element_type=jnp.float32,
    )
    lower = jnp.dot(
        w_ref[top:width, main:depth], (rows_at + LANES // 2 == cols_at).astype(jnp.bfloat16),
        preferred_element_type=jnp.float32,
    )
    own[base : base + width - top, :] = (upper[0 : width - top] + lower).astype(jnp.bfloat16)
    if 2 * top > width:
        own[base + width - top : base + top, :] = upper[width - top : top].astype(jnp.bfloat16)

    pl.semaphore_wait(barrier, len(peers))

    sends = []

    def send(src, i, q, span, recv_sem, to_img, to_seq, when=None):
        copy = pltpu.make_async_remote_copy(
            src_ref=src.at[pl.ds(*span)],
            dst_ref=wbuf.at[i, q, pl.ds(*span)],
            send_sem=send_sems.at[len(sends)],
            recv_sem=recv_sem,
            device_id={"img": to_img, "seq": to_seq},
            device_id_type=pl.DeviceIdType.MESH,
        )
        if when is None:
            copy.start()
        else:
            pl.when(when)(copy.start)
        sends.append((copy, when))

    def arrive(i, q, span, recv_sem):
        block = wbuf.at[i, q, pl.ds(*span)]
        pltpu.make_async_remote_copy(
            src_ref=block, dst_ref=block, send_sem=send_sems.at[0], recv_sem=recv_sem,
            device_id={"img": img, "seq": twin}, device_id_type=pl.DeviceIdType.MESH,
        ).wait_recv()

    slot = {A0: 0, A1: 1, B0: 2, B1: 3, B: 2}

    def get(i, q, *spans):
        for span in spans:
            arrive(i, q, span, in_sems.at[i, q, slot[span]])

    def give(src, i, q, to, *spans):
        for span in spans:
            send(src, i, q, span, in_sems.at[i, q, slot[span]], to, seq)

    def start_line(src, i, spans):
        for span in spans:
            sem = in_sems.at[i, z, slot[span]]
            send(src, i, z, span, sem, img, lax.rem(seq + 2, n_seq), z < n_z - 1)
            send(src, i, z, span, sem, img, lax.rem(seq + n_seq - 2, n_seq), z > 0)

    def relay(src, i, q, spans):
        to = z - 1 + 2 * (q < z).astype(jnp.int32)
        inside = jnp.logical_and(to >= 0, to < n_z)
        to_seq = lax.rem(2 * to + core + n_seq, n_seq)
        for span in spans:
            send(src, i, q, span, in_sems.at[i, q, slot[span]], img, to_seq, inside)

    def block_of(i, q):
        return wbuf.at[i, q]

    keep_own = pltpu.make_async_copy(own, wbuf.at[img, z], local_sem)
    keep_own.start()
    for span in (A0, A1):
        give(own, img, z, right, span)
        give(own, img, z, left, span)
        start_line(own, img, [span])
    for span in (B0, B1):
        give(own, img, z, right, span)
        give(own, img, z, left, span)
    start_line(own, img, [B])

    flag = jnp.full((1, depth * n_img), keep_ref[0])
    condition = jnp.where(flag > 0, vectors_ref[1:2, :].astype(jnp.float32), vectors_ref[2:3, :].astype(jnp.float32))
    pair = jnp.concatenate([vectors_ref[0:1, :].astype(jnp.float32), condition], axis=0).astype(jnp.bfloat16)
    row_is = lax.broadcasted_iota(jnp.int32, (2, 2 * LANES), 0)
    col_is = lax.broadcasted_iota(jnp.int32, (2, 2 * LANES), 1) // LANES
    spread[...] = lax.dot_general(
        pair, (row_is == col_is).astype(jnp.bfloat16), (((0,), (0,)), ((), ())),
        preferred_element_type=jnp.float32,
    )
    ends_upper[:, 0:token_count] = jnp.zeros((n_img * LANES, token_count), jnp.bfloat16)
    ends_lower[...] = jnp.zeros_like(ends_lower)
    for t in range(grid_rows):
        cols = slice(grid_cols * t, grid_cols * (t + 1))
        features = tokens_ref[t].astype(jnp.float32)
        mean_square = jnp.mean(features * features, axis=0, keepdims=True)
        scale = lax.rsqrt(mean_square + norm_eps)
        for i in range(n_img):
            rows = slice(depth * i, depth * (i + 1))
            hidden = (
                tokens_ref[t, rows, :].astype(jnp.float32) * scale * spread[rows, 0:LANES]
                + spread[rows, LANES:]
            ).astype(jnp.bfloat16)
            hid[main * i : main * (i + 1), cols] = hidden[0:main]
            ends_upper[LANES * i : LANES * i + tail, cols] = hidden[main:depth]
            half = LANES * i + LANES // 2
            ends_lower[half : half + tail, cols] = hidden[main:depth]

    keep_own.wait()

    def swap(n, src_ref, dst_ref):
        return pltpu.make_async_remote_copy(
            src_ref=src_ref, dst_ref=dst_ref, send_sem=swap_send.at[n], recv_sem=swap_recv.at[n],
            device_id={"img": img, "seq": twin}, device_id_type=pl.DeviceIdType.MESH,
        )

    here, there = pl.ds(0, token_count), pl.ds(token_count, token_count)
    swaps = [swap(0, hid.at[:, here], hid.at[:, there]), swap(1, ends_upper.at[:, here], ends_upper.at[:, there])]
    for copy in swaps:
        copy.start()

    def project(k):
        block = jnp.concatenate(
            [
                wbuf[i, zs[k], width * j : width * (j + 1), :]
                for i in range(n_img)
                for j in range(main_tiles)
            ],
            axis=1,
        )
        ends = jnp.concatenate([wbuf[i, zs[k], base : base + top, :] for i in range(n_img)], axis=1)
        acc = jnp.dot(block, hid[...], preferred_element_type=jnp.float32)
        acc_upper = jnp.dot(ends, ends_upper[...], preferred_element_type=jnp.float32)
        acc_lower = jnp.dot(ends[0 : width - top], ends_lower[...], preferred_element_type=jnp.float32)
        at = pl.multiple_of(mine[k] * width, width)
        first, second = acc[0:top] + acc_upper, acc[top:width] + acc_lower
        returns[k, 0:top, :] = first[:, token_count:]
        returns[k, top:width, :] = second[:, token_count:]
        copy = swap(2 + k, returns.at[k], full.at[pl.ds(at, width)])
        copy.start()
        swaps.append(copy)
        full[pl.ds(at, top), :] = first[:, 0:token_count]
        full[pl.ds(at + top, width - top), :] = second[:, 0:token_count]

    def finish(k):
        if k == 0:
            swaps[0].wait_recv()
            swaps[1].wait_recv()
            for i in range(n_img):
                half = LANES * i + LANES // 2
                ends_lower[half : half + tail, token_count:] = ends_upper[
                    LANES * i : LANES * i + tail, token_count:
                ]
        project(k)

    def side_rows(q):
        for i in (left, right, far):
            get(i, q, B)
            relay(block_of(i, q), i, q, [B])

    for k in range(n_z):
        if k + 1 < n_z:
            q = zs[k + 1]
            src = block_of(img, q)
            for span in (A0, A1):
                get(img, q, span)
                give(src, img, q, right, span)
                give(src, img, q, left, span)
                relay(src, img, q, [span])
            get(img, q, B)
            relay(src, img, q, [B])
        q = zs[k]
        from_left, from_right, from_far = block_of(left, q), block_of(right, q), block_of(far, q)
        get(left, q, A0)
        give(from_left, left, q, right, A0)
        get(right, q, A0, A1)
        give(from_right, right, q, left, A1)
        get(left, q, A1)
        if k == 0:
            get(left, q, B0)
            give(from_left, left, q, right, B0)
            get(right, q, B0, B1)
            give(from_right, right, q, left, B1)
            start_line(from_right, right, [B])
            get(left, q, B1)
            start_line(from_left, left, [B])
        elif k == 1:
            side_rows(q)
        elif k == 2:
            side_rows(q)
            side_rows(zs[3])
        get(far, q, A0, A1)
        if k == 0:
            get(far, q, B0, B1)
            start_line(from_far, far, [B])
        else:
            finish(k - 1)
    finish(n_z - 1)

    for k in range(n_z):
        rows = full.at[pl.ds(pl.multiple_of(twins[k] * width, width), width)]
        swap(2 + k, rows, rows).wait_recv()

    groups = inner // LANES
    head_of_row = lax.broadcasted_iota(jnp.int32, (LANES, LANES), 0) // HDIM
    head_of_col = lax.broadcasted_iota(jnp.int32, (LANES, LANES), 1) // HDIM
    same = (head_of_row == head_of_col).astype(jnp.float32)
    live_rows = seq * grid_rows + lax.broadcasted_iota(jnp.int32, (1, token_count), 1) // grid_cols
    live = (live_rows < rows_ref[0]).astype(jnp.float32)
    state[...] = jnp.zeros_like(state)
    by_lanes = (((1,), (1,)), ((), ()))
    by_rows = (((1,), (0,)), ((), ()))
    ones = jnp.ones((8, token_count), jnp.float32)
    for g in range(groups):
        keys = jax.nn.relu(full[inner + LANES * g : inner + LANES * (g + 1), :]) * live
        values = full[2 * inner + LANES * g : 2 * inner + LANES * (g + 1), :]
        outer = product(jnp.concatenate([values, ones], axis=0), keys, by_lanes)
        kept = outer[0:LANES] * same
        state[HDIM * g : HDIM * (g + 1), :] = kept[0:32] + kept[32:64] + kept[64:96] + kept[96:128]
        state[HDIM * groups + g : HDIM * groups + g + 1, :] = outer[LANES : LANES + 1]

    piece = state.shape[0] // n_seq

    def piece_of(ref, s):
        return ref.at[pl.ds(pl.multiple_of(s * piece, piece), piece)]

    scattered, gathered = [], []
    for d in range(1, n_seq):
        to = lax.rem(seq + d, n_seq)
        copy = pltpu.make_async_remote_copy(
            src_ref=piece_of(state, to), dst_ref=pieces.at[d - 1],
            send_sem=send_sems.at[len(sends) + d - 1], recv_sem=piece_sems.at[d - 1],
            device_id={"img": img, "seq": to}, device_id_type=pl.DeviceIdType.MESH,
        )
        copy.start()
        scattered.append(copy)
    summed = state[pl.ds(pl.multiple_of(seq * piece, piece), piece), :]
    for d in range(1, n_seq):
        scattered[d - 1].wait_recv()
        summed = summed + pieces[d - 1]
    total[pl.ds(pl.multiple_of(seq * piece, piece), piece), :] = summed
    for d in range(1, n_seq):
        copy = pltpu.make_async_remote_copy(
            src_ref=piece_of(total, seq), dst_ref=piece_of(total, seq),
            send_sem=send_sems.at[len(sends) + n_seq - 1 + d - 1], recv_sem=total_sems.at[d - 1],
            device_id={"img": img, "seq": lax.rem(seq + d, n_seq)}, device_id_type=pl.DeviceIdType.MESH,
        )
        copy.start()
        gathered.append(copy)
    for d in range(1, n_seq):
        block = piece_of(total, lax.rem(seq + n_seq - d, n_seq))
        pltpu.make_async_remote_copy(
            src_ref=block, dst_ref=block, send_sem=send_sems.at[0], recv_sem=total_sems.at[d - 1],
            device_id={"img": img, "seq": twin}, device_id_type=pl.DeviceIdType.MESH,
        ).wait_recv()

    for g in range(groups):
        queries = jax.nn.relu(full[LANES * g : LANES * (g + 1), :])
        compact = total[HDIM * g : HDIM * (g + 1), :]
        outer = jnp.concatenate([compact] * (LANES // HDIM), axis=0) * same
        key_total = total[HDIM * groups + g : HDIM * groups + g + 1, :] * same
        both = product(jnp.concatenate([outer, key_total], axis=0), queries, by_rows)
        result = (both[0:LANES] / (both[LANES:] + attn_eps) * live).astype(out_ref.dtype)
        for t in range(grid_rows):
            out_ref[t, LANES * g : LANES * (g + 1), :] = result[:, grid_cols * t : grid_cols * (t + 1)]

    for copy, when in sends:
        if when is None:
            copy.wait_send()
        else:
            pl.when(when)(copy.wait_send)
    for copy in swaps + scattered + gathered:
        copy.wait_send()


def fast_body(mesh, tokens, norm_gain, caption, null_caption, keep, bucket_rows, w_qkv):
    n_img, n_seq = mesh.shape["img"], mesh.shape["seq"]
    _, grid_rows, grid_cols, features = tokens.shape
    depth, width = w_qkv.shape
    inner = width * n_seq // 3
    token_count = grid_rows * grid_cols
    n_z = n_seq // 2
    packed = width * (depth // LANES) + half_rows(width)
    state_rows = (HDIM + 1) * (inner // LANES)
    piece = -(-state_rows // (8 * n_seq)) * 8
    dims = (n_img, n_seq, grid_rows, grid_cols, depth, width, inner)
    vmem = pl.BlockSpec(memory_space=pltpu.VMEM)
    smem = pl.BlockSpec(memory_space=pltpu.SMEM)
    dma = pltpu.SemaphoreType.DMA
    out = pl.pallas_call(
        functools.partial(kernel, dims),
        out_shape=jax.ShapeDtypeStruct((grid_rows, inner, grid_cols), jnp.bfloat16),
        in_specs=[vmem, vmem, smem, smem, vmem],
        out_specs=vmem,
        scratch_shapes=[
            pltpu.VMEM((packed, LANES), jnp.bfloat16),
            pltpu.VMEM((n_img, n_z, packed, LANES), jnp.bfloat16),
            pltpu.VMEM((n_img * (depth // LANES) * LANES, 2 * token_count), jnp.bfloat16),
            pltpu.VMEM((n_img * LANES, 2 * token_count), jnp.bfloat16),
            pltpu.VMEM((n_img * LANES, 2 * token_count), jnp.bfloat16),
            pltpu.VMEM((features, 2 * LANES), jnp.float32),
            pltpu.VMEM((n_z, width, token_count), jnp.float32),
            pltpu.VMEM((3 * inner, token_count), jnp.float32),
            pltpu.VMEM((piece * n_seq, LANES), jnp.float32),
            pltpu.VMEM((n_seq - 1, piece, LANES), jnp.float32),
            pltpu.VMEM((piece * n_seq, LANES), jnp.float32),
            dma((192,)),
            dma((n_img, n_z, 4)),
            dma((2 + n_z,)),
            dma((2 + n_z,)),
            dma((n_seq - 1,)),
            dma((n_seq - 1,)),
            dma(()),
        ],
        compiler_params=pltpu.CompilerParams(
            collective_id=0, has_side_effects=True, vmem_limit_bytes=56 * 1024 * 1024
        ),
        cost_estimate=pl.CostEstimate(
            flops=2 * token_count * features * 3 * inner, bytes_accessed=4 * token_count * features,
            transcendentals=0,
        ),
    )(
        tokens.transpose(0, 1, 3, 2).reshape(grid_rows, features, grid_cols),
        jnp.stack([norm_gain, caption[0], null_caption]), keep, bucket_rows, w_qkv.T,
    )
    return out.transpose(0, 2, 1).reshape(1, grid_rows, grid_cols, inner)


def body(tokens, norm_gain, caption, null_caption, keep, bucket_rows, w_qkv):
    grid_rows = tokens.shape[1]
    grid_cols = tokens.shape[2]
    features_count = tokens.shape[3]
    token_count = grid_rows * grid_cols
    features = tokens.reshape(token_count, features_count).astype(jnp.float32)
    mean_square = jnp.mean(features * features, axis=1, keepdims=True)
    condition = jnp.where(keep[0] > 0, caption[0], null_caption).astype(jnp.float32)
    hidden = (
        features * lax.rsqrt(mean_square + norm_eps) * norm_gain.astype(jnp.float32) + condition
    ).astype(jnp.bfloat16)
    rows_whole = lax.all_gather(w_qkv, "img", axis=0, tiled=True)
    projected = jnp.dot(
        hidden,
        lax.all_gather(rows_whole, "seq", axis=1, tiled=True),
        preferred_element_type=jnp.float32,
    )
    inner_width = projected.shape[1] // 3
    head_count = inner_width // HDIM
    grid_row = (
        lax.axis_index("seq") * grid_rows + jnp.arange(token_count, dtype=jnp.int32) // grid_cols
    )
    live_mask = (grid_row < bucket_rows[0]).astype(jnp.float32)
    queries = jax.nn.relu(projected[:, :inner_width]).reshape(token_count, head_count, HDIM)
    keys_relu = jax.nn.relu(projected[:, inner_width : 2 * inner_width]).reshape(
        token_count, head_count, HDIM
    )
    keys_relu = keys_relu * live_mask[:, None, None]
    values = projected[:, 2 * inner_width :].reshape(token_count, head_count, HDIM)
    state_outer = jnp.einsum("thd,the->hde", keys_relu, values, precision=lax.Precision.HIGHEST)
    key_total = jnp.sum(keys_relu, axis=0)
    state_outer, key_total = lax.psum((state_outer, key_total), "seq")
    numerator = jnp.einsum("thd,hde->the", queries, state_outer, precision=lax.Precision.HIGHEST)
    denominator = jnp.einsum("thd,hd->th", queries, key_total, precision=lax.Precision.HIGHEST)
    result = numerator / (denominator[:, :, None] + attn_eps) * live_mask[:, None, None]
    return result.reshape(1, grid_rows, grid_cols, inner_width).astype(jnp.bfloat16)


def solution(mesh):
    in_specs = (
        P("img", "seq", None, None),
        P(),
        P("img", None),
        P(),
        P("img"),
        P("img"),
        P("img", "seq"),
    )
    out_specs = P("img", "seq", None, None)
    plane = mesh.shape["img"] == 4 and mesh.shape["seq"] == 8
    run = functools.partial(fast_body, mesh) if plane else body
    return jax.shard_map(run, mesh=mesh, in_specs=in_specs, out_specs=out_specs, check_vma=False)
```

```python
import functools

import jax
import jax.numpy as jnp
from jax import lax
from jax.experimental import pallas as pl
from jax.experimental.pallas import tpu as pltpu
from jax.sharding import PartitionSpec as P

HDIM = 32
LANES = 128

norm_eps = 1e-06
attn_eps = 1e-06


def gray(r):
    return r + r // 2 - 2 * (r // 3)


def half_rows(width):
    return -(-width // 32) * 16


def parts_of(packed):
    units = packed // 16
    b = round(units * 0.15)
    a = units - b
    cuts = [0, (a + 1) // 2, a, a + (b + 1) // 2, units]
    cuts = [16 * c for c in cuts]

    def span(i, j):
        return (cuts[i], cuts[j] - cuts[i])

    return span(0, 2), span(0, 1), span(1, 2), span(2, 4), span(2, 3), span(3, 4)


def product(a, b, dims):
    a_high, b_high = a.astype(jnp.bfloat16), b.astype(jnp.bfloat16)
    a_low = (a - a_high.astype(jnp.float32)).astype(jnp.bfloat16)
    b_low = (b - b_high.astype(jnp.float32)).astype(jnp.bfloat16)
    rows = a.shape[0]
    first = lax.dot_general(
        jnp.concatenate([a_high, a_low], axis=0), b_high, dims, preferred_element_type=jnp.float32
    )
    return (
        first[0:rows] + first[rows:]
        + lax.dot_general(a_high, b_low, dims, preferred_element_type=jnp.float32)
    )


def kernel(
    dims,
    tokens_ref, vectors_ref, keep_ref, rows_ref, w_ref,
    out_ref,
    own, wbuf, hid, ends_upper, ends_lower, spread, returns, full, state, pieces, total,
    send_sems, in_sems, swap_send, swap_recv, sum_sems, piece_sems, total_sems, local_sem,
):
    n_img, n_seq, grid_rows, grid_cols, depth, width, inner = dims
    main_tiles = depth // LANES
    main = main_tiles * LANES
    tail = depth - main
    top = half_rows(width)
    packed = own.shape[0]
    A, A0, A1, B, B0, B1 = parts_of(packed)
    n_z = n_seq // 2
    token_count = grid_rows * grid_cols

    seq = lax.axis_index("seq")
    img = lax.axis_index("img")
    core = lax.rem(seq, 2)
    z = seq // 2
    ring = gray(img)
    right = gray(lax.rem(ring + 1, 4))
    left = gray(lax.rem(ring + 3, 4))
    far = gray(lax.rem(ring + 2, 4))
    twin = seq + 1 - 2 * core
    zs = [
        jnp.where(z == 0, 1, z),
        jnp.where(z == 0, 2, jnp.where(z == 2, 3, 2)),
        jnp.where(z < 2, 3, 1),
        jnp.zeros_like(z),
    ]
    arrivals = [jnp.where(z == 0, zs[k], zs[k + 1]) for k in range(n_z - 1)]
    mine = [2 * q + core for q in zs]
    twins = [2 * q + 1 - core for q in zs]

    barrier = pltpu.get_barrier_semaphore()
    peers = [(img, lax.rem(seq + d, n_seq)) for d in range(1, n_seq)] + [(left, seq), (right, seq)]
    for i, s in peers:
        pl.semaphore_signal(
            barrier, inc=1, device_id={"img": i, "seq": s}, device_id_type=pl.DeviceIdType.MESH
        )

    for j in range(main_tiles):
        own[width * j : width * (j + 1), :] = w_ref[:, LANES * j : LANES * (j + 1)]
    rows_at = lax.broadcasted_iota(jnp.int32, (tail, LANES), 0)
    cols_at = lax.broadcasted_iota(jnp.int32, (tail, LANES), 1)
    base = width * main_tiles
    upper = jnp.dot(
        w_ref[0:top, main:depth], (rows_at == cols_at).astype(jnp.bfloat16),
        preferred_element_type=jnp.float32,
    )
    lower = jnp.dot(
        w_ref[top:width, main:depth], (rows_at + LANES // 2 == cols_at).astype(jnp.bfloat16),
        preferred_element_type=jnp.float32,
    )
    own[base : base + width - top, :] = (upper[0 : width - top] + lower).astype(jnp.bfloat16)
    if 2 * top > width:
        own[base + width - top : base + top, :] = upper[width - top : top].astype(jnp.bfloat16)

    pl.semaphore_wait(barrier, len(peers))

    sends = []

    def send(src, i, q, span, recv_sem, to_img, to_seq, when=None):
        copy = pltpu.make_async_remote_copy(
            src_ref=src.at[pl.ds(*span)],
            dst_ref=wbuf.at[i, q, pl.ds(*span)],
            send_sem=send_sems.at[len(sends)],
            recv_sem=recv_sem,
            device_id={"img": to_img, "seq": to_seq},
            device_id_type=pl.DeviceIdType.MESH,
        )
        if when is None:
            copy.start()
        else:
            pl.when(when)(copy.start)
        sends.append((copy, when))

    def arrive(i, q, span, recv_sem):
        block = wbuf.at[i, q, pl.ds(*span)]
        pltpu.make_async_remote_copy(
            src_ref=block, dst_ref=block, send_sem=send_sems.at[0], recv_sem=recv_sem,
            device_id={"img": img, "seq": twin}, device_id_type=pl.DeviceIdType.MESH,
        ).wait_recv()

    slot = {A0: 0, A1: 1, B0: 2, B1: 3, B: 2}

    def get(i, q, *spans):
        for span in spans:
            arrive(i, q, span, in_sems.at[i, q, slot[span]])

    def give(src, i, q, to, span, when=None):
        send(src, i, q, span, in_sems.at[i, q, slot[span]], to, seq, when)

    def start_line(src, i, spans):
        for span in spans:
            sem = in_sems.at[i, z, slot[span]]
            send(src, i, z, span, sem, img, lax.rem(seq + 2, n_seq), z < n_z - 1)
            send(src, i, z, span, sem, img, lax.rem(seq + n_seq - 2, n_seq), z > 0)

    def relay(src, i, q, spans):
        to = z - 1 + 2 * (q < z).astype(jnp.int32)
        inside = jnp.logical_and(to >= 0, to < n_z)
        to_seq = lax.rem(2 * to + core + n_seq, n_seq)
        for span in spans:
            send(src, i, q, span, in_sems.at[i, q, slot[span]], img, to_seq, inside)

    def block_of(i, q):
        return wbuf.at[i, q]

    keep_own = pltpu.make_async_copy(own, wbuf.at[img, z], local_sem)
    keep_own.start()
    for span, when in ((A0, None), (A1, z > 0)):
        give(own, img, z, right, span, when)
        give(own, img, z, left, span, when)
        start_line(own, img, [span])
    for span in (B0, B1):
        give(own, img, z, right, span)
        give(own, img, z, left, span)
    start_line(own, img, [B])

    flag = jnp.full((1, depth * n_img), keep_ref[0])
    condition = jnp.where(flag > 0, vectors_ref[1:2, :].astype(jnp.float32), vectors_ref[2:3, :].astype(jnp.float32))
    pair = jnp.concatenate([vectors_ref[0:1, :].astype(jnp.float32), condition], axis=0).astype(jnp.bfloat16)
    row_is = lax.broadcasted_iota(jnp.int32, (2, 2 * LANES), 0)
    col_is = lax.broadcasted_iota(jnp.int32, (2, 2 * LANES), 1) // LANES
    spread[...] = lax.dot_general(
        pair, (row_is == col_is).astype(jnp.bfloat16), (((0,), (0,)), ((), ())),
        preferred_element_type=jnp.float32,
    )
    ends_upper[:, 0:token_count] = jnp.zeros((n_img * LANES, token_count), jnp.bfloat16)
    ends_lower[...] = jnp.zeros_like(ends_lower)
    for t in range(grid_rows):
        cols = slice(grid_cols * t, grid_cols * (t + 1))
        features = tokens_ref[t].astype(jnp.float32)
        mean_square = jnp.mean(features * features, axis=0, keepdims=True)
        scale = lax.rsqrt(mean_square + norm_eps)
        for i in range(n_img):
            rows = slice(depth * i, depth * (i + 1))
            hidden = (
                tokens_ref[t, rows, :].astype(jnp.float32) * scale * spread[rows, 0:LANES]
                + spread[rows, LANES:]
            ).astype(jnp.bfloat16)
            hid[main * i : main * (i + 1), cols] = hidden[0:main]
            ends_upper[LANES * i : LANES * i + tail, cols] = hidden[main:depth]
            half = LANES * i + LANES // 2
            ends_lower[half : half + tail, cols] = hidden[main:depth]

    keep_own.wait()

    def swap(n, src_ref, dst_ref):
        return pltpu.make_async_remote_copy(
            src_ref=src_ref, dst_ref=dst_ref, send_sem=swap_send.at[n], recv_sem=swap_recv.at[n],
            device_id={"img": img, "seq": twin}, device_id_type=pl.DeviceIdType.MESH,
        )

    here, there = pl.ds(0, token_count), pl.ds(token_count, token_count)
    swaps = [swap(0, hid.at[:, here], hid.at[:, there]), swap(1, ends_upper.at[:, here], ends_upper.at[:, there])]
    for copy in swaps:
        copy.start()

    def project(k):
        block = jnp.concatenate(
            [
                wbuf[i, zs[k], width * j : width * (j + 1), :]
                for i in range(n_img)
                for j in range(main_tiles)
            ],
            axis=1,
        )
        ends = jnp.concatenate([wbuf[i, zs[k], base : base + top, :] for i in range(n_img)], axis=1)
        acc = jnp.dot(block, hid[...], preferred_element_type=jnp.float32)
        acc_upper = jnp.dot(ends, ends_upper[...], preferred_element_type=jnp.float32)
        acc_lower = jnp.dot(ends[0 : width - top], ends_lower[...], preferred_element_type=jnp.float32)
        at = pl.multiple_of(mine[k] * width, width)
        first, second = acc[0:top] + acc_upper, acc[top:width] + acc_lower
        returns[k, 0:top, :] = first[:, token_count:]
        returns[k, top:width, :] = second[:, token_count:]
        copy = swap(2 + k, returns.at[k], full.at[pl.ds(at, width)])
        copy.start()
        swaps.append(copy)
        full[pl.ds(at, top), :] = first[:, 0:token_count]
        full[pl.ds(at + top, width - top), :] = second[:, 0:token_count]

    def finish(k):
        if k == 0:
            swaps[0].wait_recv()
            swaps[1].wait_recv()
            for i in range(n_img):
                half = LANES * i + LANES // 2
                ends_lower[half : half + tail, token_count:] = ends_upper[
                    LANES * i : LANES * i + tail, token_count:
                ]
        project(k)

    def side_rows(q):
        for i in (left, right, far):
            get(i, q, B)
            relay(block_of(i, q), i, q, [B])

    def twin_done(k):
        rows = full.at[pl.ds(pl.multiple_of(twins[k] * width, width), width)]
        swap(2 + k, rows, rows).wait_recv()

    for k in range(n_z):
        if k + 1 < n_z:
            q = arrivals[k]
            src = block_of(img, q)
            for span in (A0, A1):
                get(img, q, span)
                give(src, img, q, right, span)
                give(src, img, q, left, span)
                relay(src, img, q, [span])
            get(img, q, B)
            relay(src, img, q, [B])
        if k + 2 == n_z:
            give(own, img, z, right, A1, z == 0)
            give(own, img, z, left, A1, z == 0)
        q = zs[k]
        from_left, from_right = block_of(left, q), block_of(right, q)
        get(left, q, A0)
        give(from_left, left, q, right, A0)
        get(right, q, A0, A1)
        give(from_right, right, q, left, A1)
        get(left, q, A1)
        if k == 0:
            get(left, z, B0)
            give(block_of(left, z), left, z, right, B0)
            get(right, z, B0, B1)
            give(block_of(right, z), right, z, left, B1)
            get(left, z, B1)
            get(far, q, A0, A1)
            continue
        if k == 1:
            get(far, z, B0, B1)
            for i in (left, right, far):
                start_line(block_of(i, z), i, [B])
        side_rows(arrivals[k - 1])
        finish(k - 1)
        if k + 1 < n_z:
            get(far, q, A0, A1)

    for k in range(n_z - 1):
        twin_done(k)
    groups = inner // LANES
    head_of_row = lax.broadcasted_iota(jnp.int32, (LANES, LANES), 0) // HDIM
    head_of_col = lax.broadcasted_iota(jnp.int32, (LANES, LANES), 1) // HDIM
    same = (head_of_row == head_of_col).astype(jnp.float32)
    live_rows = seq * grid_rows + lax.broadcasted_iota(jnp.int32, (1, token_count), 1) // grid_cols
    live = (live_rows < rows_ref[0]).astype(jnp.float32)
    state[...] = jnp.zeros_like(state)
    by_lanes = (((1,), (1,)), ((), ()))
    by_rows = (((1,), (0,)), ((), ()))
    ones = jnp.ones((8, token_count), jnp.float32)
    for g in range(groups):
        keys = jax.nn.relu(full[inner + LANES * g : inner + LANES * (g + 1), :]) * live
        values = full[2 * inner + LANES * g : 2 * inner + LANES * (g + 1), :]
        outer = product(jnp.concatenate([values, ones], axis=0), keys, by_lanes)
        kept = outer[0:LANES] * same
        state[HDIM * g : HDIM * (g + 1), :] = kept[0:32] + kept[32:64] + kept[64:96] + kept[96:128]
        state[HDIM * groups + g : HDIM * groups + g + 1, :] = outer[LANES : LANES + 1]

    piece = state.shape[0] // n_seq

    def piece_of(ref, s):
        return ref.at[pl.ds(pl.multiple_of(s * piece, piece), piece)]

    scattered, gathered = [], []
    for d in range(1, n_seq):
        to = lax.rem(seq + d, n_seq)
        copy = pltpu.make_async_remote_copy(
            src_ref=piece_of(state, to), dst_ref=pieces.at[d - 1],
            send_sem=sum_sems.at[0, d - 1], recv_sem=piece_sems.at[d - 1],
            device_id={"img": img, "seq": to}, device_id_type=pl.DeviceIdType.MESH,
        )
        copy.start()
        scattered.append(copy)
    get(far, zs[n_z - 1], A0, A1)
    finish(n_z - 1)
    summed = state[pl.ds(pl.multiple_of(seq * piece, piece), piece), :]
    for d in range(1, n_seq):
        scattered[d - 1].wait_recv()
        summed = summed + pieces[d - 1]
    total[pl.ds(pl.multiple_of(seq * piece, piece), piece), :] = summed
    for d in range(1, n_seq):
        copy = pltpu.make_async_remote_copy(
            src_ref=piece_of(total, seq), dst_ref=piece_of(total, seq),
            send_sem=sum_sems.at[1, d - 1], recv_sem=total_sems.at[d - 1],
            device_id={"img": img, "seq": lax.rem(seq + d, n_seq)}, device_id_type=pl.DeviceIdType.MESH,
        )
        copy.start()
        gathered.append(copy)
    twin_done(n_z - 1)
    for d in range(1, n_seq):
        block = piece_of(total, lax.rem(seq + n_seq - d, n_seq))
        pltpu.make_async_remote_copy(
            src_ref=block, dst_ref=block, send_sem=send_sems.at[0], recv_sem=total_sems.at[d - 1],
            device_id={"img": img, "seq": twin}, device_id_type=pl.DeviceIdType.MESH,
        ).wait_recv()

    for g in range(groups):
        queries = jax.nn.relu(full[LANES * g : LANES * (g + 1), :])
        compact = total[HDIM * g : HDIM * (g + 1), :]
        outer = jnp.concatenate([compact] * (LANES // HDIM), axis=0) * same
        key_total = total[HDIM * groups + g : HDIM * groups + g + 1, :] * same
        both = product(jnp.concatenate([outer, key_total], axis=0), queries, by_rows)
        result = (both[0:LANES] / (both[LANES:] + attn_eps) * live).astype(out_ref.dtype)
        for t in range(grid_rows):
            out_ref[t, LANES * g : LANES * (g + 1), :] = result[:, grid_cols * t : grid_cols * (t + 1)]

    for copy, when in sends:
        if when is None:
            copy.wait_send()
        else:
            pl.when(when)(copy.wait_send)
    for copy in swaps + scattered + gathered:
        copy.wait_send()


def fast_body(mesh, tokens, norm_gain, caption, null_caption, keep, bucket_rows, w_qkv):
    n_img, n_seq = mesh.shape["img"], mesh.shape["seq"]
    _, grid_rows, grid_cols, features = tokens.shape
    depth, width = w_qkv.shape
    inner = width * n_seq // 3
    token_count = grid_rows * grid_cols
    n_z = n_seq // 2
    packed = width * (depth // LANES) + half_rows(width)
    state_rows = (HDIM + 1) * (inner // LANES)
    piece = -(-state_rows // (8 * n_seq)) * 8
    dims = (n_img, n_seq, grid_rows, grid_cols, depth, width, inner)
    vmem = pl.BlockSpec(memory_space=pltpu.VMEM)
    smem = pl.BlockSpec(memory_space=pltpu.SMEM)
    dma = pltpu.SemaphoreType.DMA
    out = pl.pallas_call(
        functools.partial(kernel, dims),
        out_shape=jax.ShapeDtypeStruct((grid_rows, inner, grid_cols), jnp.bfloat16),
        in_specs=[vmem, vmem, smem, smem, vmem],
        out_specs=vmem,
        scratch_shapes=[
            pltpu.VMEM((packed, LANES), jnp.bfloat16),
            pltpu.VMEM((n_img, n_z, packed, LANES), jnp.bfloat16),
            pltpu.VMEM((n_img * (depth // LANES) * LANES, 2 * token_count), jnp.bfloat16),
            pltpu.VMEM((n_img * LANES, 2 * token_count), jnp.bfloat16),
            pltpu.VMEM((n_img * LANES, 2 * token_count), jnp.bfloat16),
            pltpu.VMEM((features, 2 * LANES), jnp.float32),
            pltpu.VMEM((n_z, width, token_count), jnp.float32),
            pltpu.VMEM((3 * inner, token_count), jnp.float32),
            pltpu.VMEM((piece * n_seq, LANES), jnp.float32),
            pltpu.VMEM((n_seq - 1, piece, LANES), jnp.float32),
            pltpu.VMEM((piece * n_seq, LANES), jnp.float32),
            dma((192,)),
            dma((n_img, n_z, 4)),
            dma((2 + n_z,)),
            dma((2 + n_z,)),
            dma((2, n_seq - 1)),
            dma((n_seq - 1,)),
            dma((n_seq - 1,)),
            dma(()),
        ],
        compiler_params=pltpu.CompilerParams(
            collective_id=0, has_side_effects=True, vmem_limit_bytes=56 * 1024 * 1024
        ),
        cost_estimate=pl.CostEstimate(
            flops=2 * token_count * features * 3 * inner, bytes_accessed=4 * token_count * features,
            transcendentals=0,
        ),
    )(
        tokens.transpose(0, 1, 3, 2).reshape(grid_rows, features, grid_cols),
        jnp.stack([norm_gain, caption[0], null_caption]), keep, bucket_rows, w_qkv.T,
    )
    return out.transpose(0, 2, 1).reshape(1, grid_rows, grid_cols, inner)


def body(tokens, norm_gain, caption, null_caption, keep, bucket_rows, w_qkv):
    grid_rows = tokens.shape[1]
    grid_cols = tokens.shape[2]
    features_count = tokens.shape[3]
    token_count = grid_rows * grid_cols
    features = tokens.reshape(token_count, features_count).astype(jnp.float32)
    mean_square = jnp.mean(features * features, axis=1, keepdims=True)
    condition = jnp.where(keep[0] > 0, caption[0], null_caption).astype(jnp.float32)
    hidden = (
        features * lax.rsqrt(mean_square + norm_eps) * norm_gain.astype(jnp.float32) + condition
    ).astype(jnp.bfloat16)
    rows_whole = lax.all_gather(w_qkv, "img", axis=0, tiled=True)
    projected = jnp.dot(
        hidden,
        lax.all_gather(rows_whole, "seq", axis=1, tiled=True),
        preferred_element_type=jnp.float32,
    )
    inner_width = projected.shape[1] // 3
    head_count = inner_width // HDIM
    grid_row = (
        lax.axis_index("seq") * grid_rows + jnp.arange(token_count, dtype=jnp.int32) // grid_cols
    )
    live_mask = (grid_row < bucket_rows[0]).astype(jnp.float32)
    queries = jax.nn.relu(projected[:, :inner_width]).reshape(token_count, head_count, HDIM)
    keys_relu = jax.nn.relu(projected[:, inner_width : 2 * inner_width]).reshape(
        token_count, head_count, HDIM
    )
    keys_relu = keys_relu * live_mask[:, None, None]
    values = projected[:, 2 * inner_width :].reshape(token_count, head_count, HDIM)
    state_outer = jnp.einsum("thd,the->hde", keys_relu, values, precision=lax.Precision.HIGHEST)
    key_total = jnp.sum(keys_relu, axis=0)
    state_outer, key_total = lax.psum((state_outer, key_total), "seq")
    numerator = jnp.einsum("thd,hde->the", queries, state_outer, precision=lax.Precision.HIGHEST)
    denominator = jnp.einsum("thd,hd->th", queries, key_total, precision=lax.Precision.HIGHEST)
    result = numerator / (denominator[:, :, None] + attn_eps) * live_mask[:, None, None]
    return result.reshape(1, grid_rows, grid_cols, inner_width).astype(jnp.bfloat16)


def solution(mesh):
    in_specs = (
        P("img", "seq", None, None),
        P(),
        P("img", None),
        P(),
        P("img"),
        P("img"),
        P("img", "seq"),
    )
    out_specs = P("img", "seq", None, None)
    plane = mesh.shape["img"] == 4 and mesh.shape["seq"] == 8
    run = functools.partial(fast_body, mesh) if plane else body
    return jax.shard_map(run, mesh=mesh, in_specs=in_specs, out_specs=out_specs, check_vma=False)
```

```python
import functools

import jax
import jax.numpy as jnp
from jax import lax
from jax.experimental import pallas as pl
from jax.experimental.pallas import tpu as pltpu
from jax.sharding import PartitionSpec as P

HDIM = 32
LANES = 128

norm_eps = 1e-06
attn_eps = 1e-06


def gray(r):
    return r + r // 2 - 2 * (r // 3)


def half_rows(width):
    return -(-width // 32) * 16


def parts_of(packed):
    half = -(-packed // 32) * 16
    return (0, half), (half, packed - half)


def product(a, b, dims):
    a_high, b_high = a.astype(jnp.bfloat16), b.astype(jnp.bfloat16)
    a_low = (a - a_high.astype(jnp.float32)).astype(jnp.bfloat16)
    b_low = (b - b_high.astype(jnp.float32)).astype(jnp.bfloat16)
    rows = a.shape[0]
    first = lax.dot_general(
        jnp.concatenate([a_high, a_low], axis=0), b_high, dims, preferred_element_type=jnp.float32
    )
    return (
        first[0:rows] + first[rows:]
        + lax.dot_general(a_high, b_low, dims, preferred_element_type=jnp.float32)
    )


def kernel(
    dims,
    tokens_ref, vectors_ref, keep_ref, rows_ref, w_ref,
    out_ref,
    own, wbuf, hid, ends_upper, ends_lower, spread, returns, full, state, pieces, total,
    send_sems, in_sems, swap_send, swap_recv, sum_sems, piece_sems, total_sems, local_sem,
):
    n_img, n_seq, grid_rows, grid_cols, depth, width, inner = dims
    main_tiles = depth // LANES
    main = main_tiles * LANES
    tail = depth - main
    top = half_rows(width)
    packed = own.shape[0]
    A0, A1 = parts_of(packed)
    n_z = n_seq // 2
    token_count = grid_rows * grid_cols

    seq = lax.axis_index("seq")
    img = lax.axis_index("img")
    core = lax.rem(seq, 2)
    z = seq // 2
    ring = gray(img)
    right = gray(lax.rem(ring + 1, 4))
    left = gray(lax.rem(ring + 3, 4))
    far = gray(lax.rem(ring + 2, 4))
    twin = seq + 1 - 2 * core
    zs = [
        jnp.where(z == 0, 1, z),
        jnp.where(z == 0, 2, jnp.where(z == 2, 3, 2)),
        jnp.where(z < 2, 3, 1),
        jnp.zeros_like(z),
    ]
    arrivals = [jnp.where(z == 0, zs[k], zs[k + 1]) for k in range(n_z - 1)]
    mine = [2 * q + core for q in zs]
    twins = [2 * q + 1 - core for q in zs]

    barrier = pltpu.get_barrier_semaphore()
    peers = [(img, lax.rem(seq + d, n_seq)) for d in range(1, n_seq)] + [(left, seq), (right, seq)]
    for i, s in peers:
        pl.semaphore_signal(
            barrier, inc=1, device_id={"img": i, "seq": s}, device_id_type=pl.DeviceIdType.MESH
        )

    for j in range(main_tiles):
        own[width * j : width * (j + 1), :] = w_ref[:, LANES * j : LANES * (j + 1)]
    rows_at = lax.broadcasted_iota(jnp.int32, (tail, LANES), 0)
    cols_at = lax.broadcasted_iota(jnp.int32, (tail, LANES), 1)
    base = width * main_tiles
    upper = jnp.dot(
        w_ref[0:top, main:depth], (rows_at == cols_at).astype(jnp.bfloat16),
        preferred_element_type=jnp.float32,
    )
    lower = jnp.dot(
        w_ref[top:width, main:depth], (rows_at + LANES // 2 == cols_at).astype(jnp.bfloat16),
        preferred_element_type=jnp.float32,
    )
    own[base : base + width - top, :] = (upper[0 : width - top] + lower).astype(jnp.bfloat16)
    if 2 * top > width:
        own[base + width - top : base + top, :] = upper[width - top : top].astype(jnp.bfloat16)

    pl.semaphore_wait(barrier, len(peers))

    sends = []

    def send(src, i, q, span, recv_sem, to_img, to_seq, when=None):
        copy = pltpu.make_async_remote_copy(
            src_ref=src.at[pl.ds(*span)],
            dst_ref=wbuf.at[i, q, pl.ds(*span)],
            send_sem=send_sems.at[len(sends)],
            recv_sem=recv_sem,
            device_id={"img": to_img, "seq": to_seq},
            device_id_type=pl.DeviceIdType.MESH,
        )
        if when is None:
            copy.start()
        else:
            pl.when(when)(copy.start)
        sends.append((copy, when))

    def arrive(i, q, span, recv_sem):
        block = wbuf.at[i, q, pl.ds(*span)]
        pltpu.make_async_remote_copy(
            src_ref=block, dst_ref=block, send_sem=send_sems.at[0], recv_sem=recv_sem,
            device_id={"img": img, "seq": twin}, device_id_type=pl.DeviceIdType.MESH,
        ).wait_recv()

    slot = {A0: 0, A1: 1}

    def get(i, q, *spans):
        for span in spans:
            arrive(i, q, span, in_sems.at[i, q, slot[span]])

    def give(src, i, q, to, span, when=None):
        send(src, i, q, span, in_sems.at[i, q, slot[span]], to, seq, when)

    def start_line(src, i, spans):
        for span in spans:
            sem = in_sems.at[i, z, slot[span]]
            send(src, i, z, span, sem, img, lax.rem(seq + 2, n_seq), z < n_z - 1)
            send(src, i, z, span, sem, img, lax.rem(seq + n_seq - 2, n_seq), z > 0)

    def relay(src, i, q, spans):
        to = z - 1 + 2 * (q < z).astype(jnp.int32)
        inside = jnp.logical_and(to >= 0, to < n_z)
        to_seq = lax.rem(2 * to + core + n_seq, n_seq)
        for span in spans:
            send(src, i, q, span, in_sems.at[i, q, slot[span]], img, to_seq, inside)

    def block_of(i, q):
        return wbuf.at[i, q]

    keep_own = pltpu.make_async_copy(own, wbuf.at[img, z], local_sem)
    keep_own.start()
    for span, when in ((A0, None), (A1, z > 0)):
        give(own, img, z, right, span, when)
        give(own, img, z, left, span, when)
        start_line(own, img, [span])

    flag = jnp.full((1, depth * n_img), keep_ref[0])
    condition = jnp.where(flag > 0, vectors_ref[1:2, :].astype(jnp.float32), vectors_ref[2:3, :].astype(jnp.float32))
    pair = jnp.concatenate([vectors_ref[0:1, :].astype(jnp.float32), condition], axis=0).astype(jnp.bfloat16)
    row_is = lax.broadcasted_iota(jnp.int32, (2, 2 * LANES), 0)
    col_is = lax.broadcasted_iota(jnp.int32, (2, 2 * LANES), 1) // LANES
    spread[...] = lax.dot_general(
        pair, (row_is == col_is).astype(jnp.bfloat16), (((0,), (0,)), ((), ())),
        preferred_element_type=jnp.float32,
    )
    ends_upper[:, 0:token_count] = jnp.zeros((n_img * LANES, token_count), jnp.bfloat16)
    ends_lower[...] = jnp.zeros_like(ends_lower)
    for t in range(grid_rows):
        cols = slice(grid_cols * t, grid_cols * (t + 1))
        features = tokens_ref[t].astype(jnp.float32)
        mean_square = jnp.mean(features * features, axis=0, keepdims=True)
        scale = lax.rsqrt(mean_square + norm_eps)
        for i in range(n_img):
            rows = slice(depth * i, depth * (i + 1))
            hidden = (
                tokens_ref[t, rows, :].astype(jnp.float32) * scale * spread[rows, 0:LANES]
                + spread[rows, LANES:]
            ).astype(jnp.bfloat16)
            hid[main * i : main * (i + 1), cols] = hidden[0:main]
            ends_upper[LANES * i : LANES * i + tail, cols] = hidden[main:depth]
            half = LANES * i + LANES // 2
            ends_lower[half : half + tail, cols] = hidden[main:depth]

    keep_own.wait()

    def swap(n, src_ref, dst_ref):
        return pltpu.make_async_remote_copy(
            src_ref=src_ref, dst_ref=dst_ref, send_sem=swap_send.at[n], recv_sem=swap_recv.at[n],
            device_id={"img": img, "seq": twin}, device_id_type=pl.DeviceIdType.MESH,
        )

    here, there = pl.ds(0, token_count), pl.ds(token_count, token_count)
    swaps = [swap(0, hid.at[:, here], hid.at[:, there]), swap(1, ends_upper.at[:, here], ends_upper.at[:, there])]
    for copy in swaps:
        copy.start()

    def project(k):
        block = jnp.concatenate(
            [
                wbuf[i, zs[k], width * j : width * (j + 1), :]
                for i in range(n_img)
                for j in range(main_tiles)
            ],
            axis=1,
        )
        ends = jnp.concatenate([wbuf[i, zs[k], base : base + top, :] for i in range(n_img)], axis=1)
        acc = jnp.dot(block, hid[...], preferred_element_type=jnp.float32)
        acc_upper = jnp.dot(ends, ends_upper[...], preferred_element_type=jnp.float32)
        acc_lower = jnp.dot(ends[0 : width - top], ends_lower[...], preferred_element_type=jnp.float32)
        at = pl.multiple_of(mine[k] * width, width)
        first, second = acc[0:top] + acc_upper, acc[top:width] + acc_lower
        returns[k, 0:top, :] = first[:, token_count:]
        returns[k, top:width, :] = second[:, token_count:]
        copy = swap(2 + k, returns.at[k], full.at[pl.ds(at, width)])
        copy.start()
        swaps.append(copy)
        full[pl.ds(at, top), :] = first[:, 0:token_count]
        full[pl.ds(at + top, width - top), :] = second[:, 0:token_count]

    def finish(k):
        if k == 0:
            swaps[0].wait_recv()
            swaps[1].wait_recv()
            for i in range(n_img):
                half = LANES * i + LANES // 2
                ends_lower[half : half + tail, token_count:] = ends_upper[
                    LANES * i : LANES * i + tail, token_count:
                ]
        project(k)

    def twin_done(k):
        rows = full.at[pl.ds(pl.multiple_of(twins[k] * width, width), width)]
        swap(2 + k, rows, rows).wait_recv()

    def pass_on(k):
        q = arrivals[k]
        src = block_of(img, q)
        for span in (A0, A1):
            get(img, q, span)
            give(src, img, q, right, span)
            give(src, img, q, left, span)
            relay(src, img, q, [span])

    def go_round(k):
        q = zs[k]
        from_left, from_right = block_of(left, q), block_of(right, q)
        get(left, q, A0)
        give(from_left, left, q, right, A0)
        get(right, q, A0, A1)
        give(from_right, right, q, left, A1)
        get(left, q, A1)

    pass_on(0)
    for k in range(n_z - 1):
        go_round(k)
        if k + 2 < n_z:
            pass_on(k + 1)
        if k + 3 == n_z:
            give(own, img, z, right, A1, z == 0)
            give(own, img, z, left, A1, z == 0)
        if k > 0:
            finish(k - 1)
        get(far, zs[k], A0, A1)
    finish(n_z - 2)

    for k in range(n_z - 1):
        twin_done(k)
    groups = inner // LANES
    head_of_row = lax.broadcasted_iota(jnp.int32, (LANES, LANES), 0) // HDIM
    head_of_col = lax.broadcasted_iota(jnp.int32, (LANES, LANES), 1) // HDIM
    same = (head_of_row == head_of_col).astype(jnp.float32)
    live_rows = seq * grid_rows + lax.broadcasted_iota(jnp.int32, (1, token_count), 1) // grid_cols
    live = (live_rows < rows_ref[0]).astype(jnp.float32)
    state[...] = jnp.zeros_like(state)
    by_lanes = (((1,), (1,)), ((), ()))
    by_rows = (((1,), (0,)), ((), ()))
    ones = jnp.ones((8, token_count), jnp.float32)
    for g in range(groups):
        keys = jax.nn.relu(full[inner + LANES * g : inner + LANES * (g + 1), :]) * live
        values = full[2 * inner + LANES * g : 2 * inner + LANES * (g + 1), :]
        outer = product(jnp.concatenate([values, ones], axis=0), keys, by_lanes)
        kept = outer[0:LANES] * same
        state[HDIM * g : HDIM * (g + 1), :] = kept[0:32] + kept[32:64] + kept[64:96] + kept[96:128]
        state[HDIM * groups + g : HDIM * groups + g + 1, :] = outer[LANES : LANES + 1]

    piece = state.shape[0] // n_seq

    def piece_of(ref, s):
        return ref.at[pl.ds(pl.multiple_of(s * piece, piece), piece)]

    scattered, gathered = [], []
    for d in range(1, n_seq):
        to = lax.rem(seq + d, n_seq)
        copy = pltpu.make_async_remote_copy(
            src_ref=piece_of(state, to), dst_ref=pieces.at[d - 1],
            send_sem=sum_sems.at[0, d - 1], recv_sem=piece_sems.at[d - 1],
            device_id={"img": img, "seq": to}, device_id_type=pl.DeviceIdType.MESH,
        )
        copy.start()
        scattered.append(copy)
    go_round(n_z - 1)
    get(far, zs[n_z - 1], A0, A1)
    finish(n_z - 1)
    summed = state[pl.ds(pl.multiple_of(seq * piece, piece), piece), :]
    for d in range(1, n_seq):
        scattered[d - 1].wait_recv()
        summed = summed + pieces[d - 1]
    total[pl.ds(pl.multiple_of(seq * piece, piece), piece), :] = summed
    for d in range(1, n_seq):
        copy = pltpu.make_async_remote_copy(
            src_ref=piece_of(total, seq), dst_ref=piece_of(total, seq),
            send_sem=sum_sems.at[1, d - 1], recv_sem=total_sems.at[d - 1],
            device_id={"img": img, "seq": lax.rem(seq + d, n_seq)}, device_id_type=pl.DeviceIdType.MESH,
        )
        copy.start()
        gathered.append(copy)
    twin_done(n_z - 1)
    for d in range(1, n_seq):
        block = piece_of(total, lax.rem(seq + n_seq - d, n_seq))
        pltpu.make_async_remote_copy(
            src_ref=block, dst_ref=block, send_sem=send_sems.at[0], recv_sem=total_sems.at[d - 1],
            device_id={"img": img, "seq": twin}, device_id_type=pl.DeviceIdType.MESH,
        ).wait_recv()

    for g in range(groups):
        queries = jax.nn.relu(full[LANES * g : LANES * (g + 1), :])
        compact = total[HDIM * g : HDIM * (g + 1), :]
        outer = jnp.concatenate([compact] * (LANES // HDIM), axis=0) * same
        key_total = total[HDIM * groups + g : HDIM * groups + g + 1, :] * same
        both = product(jnp.concatenate([outer, key_total], axis=0), queries, by_rows)
        result = (both[0:LANES] / (both[LANES:] + attn_eps) * live).astype(out_ref.dtype)
        for t in range(grid_rows):
            out_ref[t, LANES * g : LANES * (g + 1), :] = result[:, grid_cols * t : grid_cols * (t + 1)]

    for copy, when in sends:
        if when is None:
            copy.wait_send()
        else:
            pl.when(when)(copy.wait_send)
    for copy in swaps + scattered + gathered:
        copy.wait_send()


def fast_body(mesh, tokens, norm_gain, caption, null_caption, keep, bucket_rows, w_qkv):
    n_img, n_seq = mesh.shape["img"], mesh.shape["seq"]
    _, grid_rows, grid_cols, features = tokens.shape
    depth, width = w_qkv.shape
    inner = width * n_seq // 3
    token_count = grid_rows * grid_cols
    n_z = n_seq // 2
    packed = width * (depth // LANES) + half_rows(width)
    state_rows = (HDIM + 1) * (inner // LANES)
    piece = -(-state_rows // (8 * n_seq)) * 8
    dims = (n_img, n_seq, grid_rows, grid_cols, depth, width, inner)
    vmem = pl.BlockSpec(memory_space=pltpu.VMEM)
    smem = pl.BlockSpec(memory_space=pltpu.SMEM)
    dma = pltpu.SemaphoreType.DMA
    out = pl.pallas_call(
        functools.partial(kernel, dims),
        out_shape=jax.ShapeDtypeStruct((grid_rows, inner, grid_cols), jnp.bfloat16),
        in_specs=[vmem, vmem, smem, smem, vmem],
        out_specs=vmem,
        scratch_shapes=[
            pltpu.VMEM((packed, LANES), jnp.bfloat16),
            pltpu.VMEM((n_img, n_z, packed, LANES), jnp.bfloat16),
            pltpu.VMEM((n_img * (depth // LANES) * LANES, 2 * token_count), jnp.bfloat16),
            pltpu.VMEM((n_img * LANES, 2 * token_count), jnp.bfloat16),
            pltpu.VMEM((n_img * LANES, 2 * token_count), jnp.bfloat16),
            pltpu.VMEM((features, 2 * LANES), jnp.float32),
            pltpu.VMEM((n_z, width, token_count), jnp.float32),
            pltpu.VMEM((3 * inner, token_count), jnp.float32),
            pltpu.VMEM((piece * n_seq, LANES), jnp.float32),
            pltpu.VMEM((n_seq - 1, piece, LANES), jnp.float32),
            pltpu.VMEM((piece * n_seq, LANES), jnp.float32),
            dma((192,)),
            dma((n_img, n_z, 2)),
            dma((2 + n_z,)),
            dma((2 + n_z,)),
            dma((2, n_seq - 1)),
            dma((n_seq - 1,)),
            dma((n_seq - 1,)),
            dma(()),
        ],
        compiler_params=pltpu.CompilerParams(
            collective_id=0, has_side_effects=True, vmem_limit_bytes=56 * 1024 * 1024
        ),
        cost_estimate=pl.CostEstimate(
            flops=2 * token_count * features * 3 * inner, bytes_accessed=4 * token_count * features,
            transcendentals=0,
        ),
    )(
        tokens.transpose(0, 1, 3, 2).reshape(grid_rows, features, grid_cols),
        jnp.stack([norm_gain, caption[0], null_caption]), keep, bucket_rows, w_qkv.T,
    )
    return out.transpose(0, 2, 1).reshape(1, grid_rows, grid_cols, inner)


def body(tokens, norm_gain, caption, null_caption, keep, bucket_rows, w_qkv):
    grid_rows = tokens.shape[1]
    grid_cols = tokens.shape[2]
    features_count = tokens.shape[3]
    token_count = grid_rows * grid_cols
    features = tokens.reshape(token_count, features_count).astype(jnp.float32)
    mean_square = jnp.mean(features * features, axis=1, keepdims=True)
    condition = jnp.where(keep[0] > 0, caption[0], null_caption).astype(jnp.float32)
    hidden = (
        features * lax.rsqrt(mean_square + norm_eps) * norm_gain.astype(jnp.float32) + condition
    ).astype(jnp.bfloat16)
    rows_whole = lax.all_gather(w_qkv, "img", axis=0, tiled=True)
    projected = jnp.dot(
        hidden,
        lax.all_gather(rows_whole, "seq", axis=1, tiled=True),
        preferred_element_type=jnp.float32,
    )
    inner_width = projected.shape[1] // 3
    head_count = inner_width // HDIM
    grid_row = (
        lax.axis_index("seq") * grid_rows + jnp.arange(token_count, dtype=jnp.int32) // grid_cols
    )
    live_mask = (grid_row < bucket_rows[0]).astype(jnp.float32)
    queries = jax.nn.relu(projected[:, :inner_width]).reshape(token_count, head_count, HDIM)
    keys_relu = jax.nn.relu(projected[:, inner_width : 2 * inner_width]).reshape(
        token_count, head_count, HDIM
    )
    keys_relu = keys_relu * live_mask[:, None, None]
    values = projected[:, 2 * inner_width :].reshape(token_count, head_count, HDIM)
    state_outer = jnp.einsum("thd,the->hde", keys_relu, values, precision=lax.Precision.HIGHEST)
    key_total = jnp.sum(keys_relu, axis=0)
    state_outer, key_total = lax.psum((state_outer, key_total), "seq")
    numerator = jnp.einsum("thd,hde->the", queries, state_outer, precision=lax.Precision.HIGHEST)
    denominator = jnp.einsum("thd,hd->th", queries, key_total, precision=lax.Precision.HIGHEST)
    result = numerator / (denominator[:, :, None] + attn_eps) * live_mask[:, None, None]
    return result.reshape(1, grid_rows, grid_cols, inner_width).astype(jnp.bfloat16)


def solution(mesh):
    in_specs = (
        P("img", "seq", None, None),
        P(),
        P("img", None),
        P(),
        P("img"),
        P("img"),
        P("img", "seq"),
    )
    out_specs = P("img", "seq", None, None)
    plane = mesh.shape["img"] == 4 and mesh.shape["seq"] == 8
    run = functools.partial(fast_body, mesh) if plane else body
    return jax.shard_map(run, mesh=mesh, in_specs=in_specs, out_specs=out_specs, check_vma=False)
```

```python
import functools

import jax
import jax.numpy as jnp
from jax import lax
from jax.experimental import pallas as pl
from jax.experimental.pallas import tpu as pltpu
from jax.sharding import PartitionSpec as P

HDIM = 32
LANES = 128

norm_eps = 1e-06
attn_eps = 1e-06


def gray(r):
    return r + r // 2 - 2 * (r // 3)


def half_rows(width):
    return -(-width // 32) * 16


def parts_of(packed):
    units = packed // 16
    b = round(units * 0.15)
    a = units - b
    cuts = [0, (a + 1) // 2, a, a + (b + 1) // 2, units]
    cuts = [16 * c for c in cuts]

    def span(i, j):
        return (cuts[i], cuts[j] - cuts[i])

    return span(0, 2), span(0, 1), span(1, 2), span(2, 4), span(2, 3), span(3, 4)


def product(a, b, dims):
    a_high, b_high = a.astype(jnp.bfloat16), b.astype(jnp.bfloat16)
    a_low = (a - a_high.astype(jnp.float32)).astype(jnp.bfloat16)
    b_low = (b - b_high.astype(jnp.float32)).astype(jnp.bfloat16)
    rows = a.shape[0]
    first = lax.dot_general(
        jnp.concatenate([a_high, a_low], axis=0), b_high, dims, preferred_element_type=jnp.float32
    )
    return (
        first[0:rows] + first[rows:]
        + lax.dot_general(a_high, b_low, dims, preferred_element_type=jnp.float32)
    )


def kernel(
    dims,
    tokens_ref, vectors_ref, keep_ref, rows_ref, w_ref,
    out_ref,
    own, wbuf, hid, ends_upper, ends_lower, spread, returns, full, state, pieces, total,
    send_sems, in_sems, swap_send, swap_recv, sum_sems, piece_sems, total_sems, local_sem,
):
    n_img, n_seq, grid_rows, grid_cols, depth, width, inner = dims
    main_tiles = depth // LANES
    main = main_tiles * LANES
    tail = depth - main
    top = half_rows(width)
    packed = own.shape[0]
    A, A0, A1, B, B0, B1 = parts_of(packed)
    n_z = n_seq // 2
    token_count = grid_rows * grid_cols

    seq = lax.axis_index("seq")
    img = lax.axis_index("img")
    core = lax.rem(seq, 2)
    z = seq // 2
    ring = gray(img)
    right = gray(lax.rem(ring + 1, 4))
    left = gray(lax.rem(ring + 3, 4))
    far = gray(lax.rem(ring + 2, 4))
    twin = seq + 1 - 2 * core
    zs = [
        jnp.where(z == 0, 1, z),
        jnp.where(z == 0, 2, jnp.where(z == 2, 3, 2)),
        jnp.where(z < 2, 3, 1),
        jnp.zeros_like(z),
    ]
    arrivals = [jnp.where(z == 0, zs[k], zs[k + 1]) for k in range(n_z - 1)]
    mine = [2 * q + core for q in zs]
    twins = [2 * q + 1 - core for q in zs]

    barrier = pltpu.get_barrier_semaphore()
    peers = [(img, lax.rem(seq + d, n_seq)) for d in range(1, n_seq)] + [(left, seq), (right, seq)]
    for i, s in peers:
        pl.semaphore_signal(
            barrier, inc=1, device_id={"img": i, "seq": s}, device_id_type=pl.DeviceIdType.MESH
        )

    for j in range(main_tiles):
        own[width * j : width * (j + 1), :] = w_ref[:, LANES * j : LANES * (j + 1)]
    rows_at = lax.broadcasted_iota(jnp.int32, (tail, LANES), 0)
    cols_at = lax.broadcasted_iota(jnp.int32, (tail, LANES), 1)
    base = width * main_tiles
    upper = jnp.dot(
        w_ref[0:top, main:depth], (rows_at == cols_at).astype(jnp.bfloat16),
        preferred_element_type=jnp.float32,
    )
    lower = jnp.dot(
        w_ref[top:width, main:depth], (rows_at + LANES // 2 == cols_at).astype(jnp.bfloat16),
        preferred_element_type=jnp.float32,
    )
    own[base : base + width - top, :] = (upper[0 : width - top] + lower).astype(jnp.bfloat16)
    if 2 * top > width:
        own[base + width - top : base + top, :] = upper[width - top : top].astype(jnp.bfloat16)

    pl.semaphore_wait(barrier, len(peers))

    sends = []

    def send(src, i, q, span, recv_sem, to_img, to_seq, when=None):
        copy = pltpu.make_async_remote_copy(
            src_ref=src.at[pl.ds(*span)],
            dst_ref=wbuf.at[i, q, pl.ds(*span)],
            send_sem=send_sems.at[len(sends)],
            recv_sem=recv_sem,
            device_id={"img": to_img, "seq": to_seq},
            device_id_type=pl.DeviceIdType.MESH,
        )
        if when is None:
            copy.start()
        else:
            pl.when(when)(copy.start)
        sends.append((copy, when))

    def arrive(i, q, span, recv_sem):
        block = wbuf.at[i, q, pl.ds(*span)]
        pltpu.make_async_remote_copy(
            src_ref=block, dst_ref=block, send_sem=send_sems.at[0], recv_sem=recv_sem,
            device_id={"img": img, "seq": twin}, device_id_type=pl.DeviceIdType.MESH,
        ).wait_recv()

    slot = {A0: 0, A1: 1, B0: 2, B1: 3, B: 2}

    def get(i, q, *spans):
        for span in spans:
            arrive(i, q, span, in_sems.at[i, q, slot[span]])

    def give(src, i, q, to, span, when=None):
        send(src, i, q, span, in_sems.at[i, q, slot[span]], to, seq, when)

    def start_line(src, i, spans):
        for span in spans:
            sem = in_sems.at[i, z, slot[span]]
            send(src, i, z, span, sem, img, lax.rem(seq + 2, n_seq), z < n_z - 1)
            send(src, i, z, span, sem, img, lax.rem(seq + n_seq - 2, n_seq), z > 0)

    def relay(src, i, q, spans):
        to = z - 1 + 2 * (q < z).astype(jnp.int32)
        inside = jnp.logical_and(to >= 0, to < n_z)
        to_seq = lax.rem(2 * to + core + n_seq, n_seq)
        for span in spans:
            send(src, i, q, span, in_sems.at[i, q, slot[span]], img, to_seq, inside)

    def block_of(i, q):
        return wbuf.at[i, q]

    keep_own = pltpu.make_async_copy(own, wbuf.at[img, z], local_sem)
    keep_own.start()
    for span, when in ((A0, None), (A1, z > 0)):
        give(own, img, z, right, span, when)
        give(own, img, z, left, span, when)
        start_line(own, img, [span])
    for span in (B0, B1):
        give(own, img, z, right, span)
        give(own, img, z, left, span)
    start_line(own, img, [B])

    flag = jnp.full((1, depth * n_img), keep_ref[0])
    condition = jnp.where(flag > 0, vectors_ref[1:2, :].astype(jnp.float32), vectors_ref[2:3, :].astype(jnp.float32))
    pair = jnp.concatenate([vectors_ref[0:1, :].astype(jnp.float32), condition], axis=0).astype(jnp.bfloat16)
    row_is = lax.broadcasted_iota(jnp.int32, (2, 2 * LANES), 0)
    col_is = lax.broadcasted_iota(jnp.int32, (2, 2 * LANES), 1) // LANES
    spread[...] = lax.dot_general(
        pair, (row_is == col_is).astype(jnp.bfloat16), (((0,), (0,)), ((), ())),
        preferred_element_type=jnp.float32,
    )
    ends_upper[:, 0:token_count] = jnp.zeros((n_img * LANES, token_count), jnp.bfloat16)
    ends_lower[...] = jnp.zeros_like(ends_lower)
    for t in range(grid_rows):
        cols = slice(grid_cols * t, grid_cols * (t + 1))
        features = tokens_ref[t].astype(jnp.float32)
        mean_square = jnp.mean(features * features, axis=0, keepdims=True)
        scale = lax.rsqrt(mean_square + norm_eps)
        for i in range(n_img):
            rows = slice(depth * i, depth * (i + 1))
            hidden = (
                tokens_ref[t, rows, :].astype(jnp.float32) * scale * spread[rows, 0:LANES]
                + spread[rows, LANES:]
            ).astype(jnp.bfloat16)
            hid[main * i : main * (i + 1), cols] = hidden[0:main]
            ends_upper[LANES * i : LANES * i + tail, cols] = hidden[main:depth]
            half = LANES * i + LANES // 2
            ends_lower[half : half + tail, cols] = hidden[main:depth]

    keep_own.wait()

    def swap(n, src_ref, dst_ref):
        return pltpu.make_async_remote_copy(
            src_ref=src_ref, dst_ref=dst_ref, send_sem=swap_send.at[n], recv_sem=swap_recv.at[n],
            device_id={"img": img, "seq": twin}, device_id_type=pl.DeviceIdType.MESH,
        )

    here, there = pl.ds(0, token_count), pl.ds(token_count, token_count)
    swaps = [swap(0, hid.at[:, here], hid.at[:, there]), swap(1, ends_upper.at[:, here], ends_upper.at[:, there])]
    for copy in swaps:
        copy.start()

    def project(k):
        block = jnp.concatenate(
            [
                wbuf[i, zs[k], width * j : width * (j + 1), :]
                for i in range(n_img)
                for j in range(main_tiles)
            ],
            axis=1,
        )
        ends = jnp.concatenate([wbuf[i, zs[k], base : base + top, :] for i in range(n_img)], axis=1)
        acc = jnp.dot(block, hid[...], preferred_element_type=jnp.float32)
        acc_upper = jnp.dot(ends, ends_upper[...], preferred_element_type=jnp.float32)
        acc_lower = jnp.dot(ends[0 : width - top], ends_lower[...], preferred_element_type=jnp.float32)
        at = pl.multiple_of(mine[k] * width, width)
        first, second = acc[0:top] + acc_upper, acc[top:width] + acc_lower
        returns[k, 0:top, :] = first[:, token_count:]
        returns[k, top:width, :] = second[:, token_count:]
        copy = swap(2 + k, returns.at[k], full.at[pl.ds(at, width)])
        copy.start()
        swaps.append(copy)
        full[pl.ds(at, top), :] = first[:, 0:token_count]
        full[pl.ds(at + top, width - top), :] = second[:, 0:token_count]

    def finish(k):
        if k == 0:
            swaps[0].wait_recv()
            swaps[1].wait_recv()
            for i in range(n_img):
                half = LANES * i + LANES // 2
                ends_lower[half : half + tail, token_count:] = ends_upper[
                    LANES * i : LANES * i + tail, token_count:
                ]
        project(k)

    def side_rows(q):
        for i in (left, right, far):
            get(i, q, B)
            relay(block_of(i, q), i, q, [B])

    def twin_done(k):
        rows = full.at[pl.ds(pl.multiple_of(twins[k] * width, width), width)]
        swap(2 + k, rows, rows).wait_recv()

    def pass_on(k):
        q = arrivals[k]
        src = block_of(img, q)
        for span in (A0, A1):
            get(img, q, span)
            give(src, img, q, right, span)
            give(src, img, q, left, span)
            relay(src, img, q, [span])
        get(img, q, B)
        relay(src, img, q, [B])

    def go_round(k):
        q = zs[k]
        from_left, from_right = block_of(left, q), block_of(right, q)
        get(left, q, A0)
        give(from_left, left, q, right, A0)
        get(right, q, A0, A1)
        give(from_right, right, q, left, A1)
        get(left, q, A1)

    pass_on(0)
    for k in range(n_z - 1):
        go_round(k)
        if k == 0:
            get(left, z, B0)
            give(block_of(left, z), left, z, right, B0)
            get(right, z, B0, B1)
            give(block_of(right, z), right, z, left, B1)
            get(left, z, B1)
        if k + 2 < n_z:
            pass_on(k + 1)
        if k + 3 == n_z:
            give(own, img, z, right, A1, z == 0)
            give(own, img, z, left, A1, z == 0)
        if k == 1:
            get(far, z, B0, B1)
            for i in (left, right, far):
                start_line(block_of(i, z), i, [B])
        if k > 0:
            side_rows(arrivals[k - 1])
            finish(k - 1)
        get(far, zs[k], A0, A1)
    side_rows(arrivals[n_z - 2])
    finish(n_z - 2)

    for k in range(n_z - 1):
        twin_done(k)
    groups = inner // LANES
    head_of_row = lax.broadcasted_iota(jnp.int32, (LANES, LANES), 0) // HDIM
    head_of_col = lax.broadcasted_iota(jnp.int32, (LANES, LANES), 1) // HDIM
    same = (head_of_row == head_of_col).astype(jnp.float32)
    live_rows = seq * grid_rows + lax.broadcasted_iota(jnp.int32, (1, token_count), 1) // grid_cols
    live = (live_rows < rows_ref[0]).astype(jnp.float32)
    state[...] = jnp.zeros_like(state)
    by_lanes = (((1,), (1,)), ((), ()))
    by_rows = (((1,), (0,)), ((), ()))
    ones = jnp.ones((8, token_count), jnp.float32)
    for g in range(groups):
        keys = jax.nn.relu(full[inner + LANES * g : inner + LANES * (g + 1), :]) * live
        values = full[2 * inner + LANES * g : 2 * inner + LANES * (g + 1), :]
        outer = product(jnp.concatenate([values, ones], axis=0), keys, by_lanes)
        kept = outer[0:LANES] * same
        state[HDIM * g : HDIM * (g + 1), :] = kept[0:32] + kept[32:64] + kept[64:96] + kept[96:128]
        state[HDIM * groups + g : HDIM * groups + g + 1, :] = outer[LANES : LANES + 1]

    piece = state.shape[0] // n_seq

    def piece_of(ref, s):
        return ref.at[pl.ds(pl.multiple_of(s * piece, piece), piece)]

    scattered, gathered = [], []
    for d in range(1, n_seq):
        to = lax.rem(seq + d, n_seq)
        copy = pltpu.make_async_remote_copy(
            src_ref=piece_of(state, to), dst_ref=pieces.at[d - 1],
            send_sem=sum_sems.at[0, d - 1], recv_sem=piece_sems.at[d - 1],
            device_id={"img": img, "seq": to}, device_id_type=pl.DeviceIdType.MESH,
        )
        copy.start()
        scattered.append(copy)
    go_round(n_z - 1)
    get(far, zs[n_z - 1], A0, A1)
    finish(n_z - 1)
    summed = state[pl.ds(pl.multiple_of(seq * piece, piece), piece), :]
    for d in range(1, n_seq):
        scattered[d - 1].wait_recv()
        summed = summed + pieces[d - 1]
    total[pl.ds(pl.multiple_of(seq * piece, piece), piece), :] = summed
    for d in range(1, n_seq):
        copy = pltpu.make_async_remote_copy(
            src_ref=piece_of(total, seq), dst_ref=piece_of(total, seq),
            send_sem=sum_sems.at[1, d - 1], recv_sem=total_sems.at[d - 1],
            device_id={"img": img, "seq": lax.rem(seq + d, n_seq)}, device_id_type=pl.DeviceIdType.MESH,
        )
        copy.start()
        gathered.append(copy)
    twin_done(n_z - 1)
    for d in range(1, n_seq):
        block = piece_of(total, lax.rem(seq + n_seq - d, n_seq))
        pltpu.make_async_remote_copy(
            src_ref=block, dst_ref=block, send_sem=send_sems.at[0], recv_sem=total_sems.at[d - 1],
            device_id={"img": img, "seq": twin}, device_id_type=pl.DeviceIdType.MESH,
        ).wait_recv()

    for g in range(groups):
        queries = jax.nn.relu(full[LANES * g : LANES * (g + 1), :])
        compact = total[HDIM * g : HDIM * (g + 1), :]
        outer = jnp.concatenate([compact] * (LANES // HDIM), axis=0) * same
        key_total = total[HDIM * groups + g : HDIM * groups + g + 1, :] * same
        both = product(jnp.concatenate([outer, key_total], axis=0), queries, by_rows)
        result = (both[0:LANES] / (both[LANES:] + attn_eps) * live).astype(out_ref.dtype)
        for t in range(grid_rows):
            out_ref[t, LANES * g : LANES * (g + 1), :] = result[:, grid_cols * t : grid_cols * (t + 1)]

    for copy, when in sends:
        if when is None:
            copy.wait_send()
        else:
            pl.when(when)(copy.wait_send)
    for copy in swaps + scattered + gathered:
        copy.wait_send()


def fast_body(mesh, tokens, norm_gain, caption, null_caption, keep, bucket_rows, w_qkv):
    n_img, n_seq = mesh.shape["img"], mesh.shape["seq"]
    _, grid_rows, grid_cols, features = tokens.shape
    depth, width = w_qkv.shape
    inner = width * n_seq // 3
    token_count = grid_rows * grid_cols
    n_z = n_seq // 2
    packed = width * (depth // LANES) + half_rows(width)
    state_rows = (HDIM + 1) * (inner // LANES)
    piece = -(-state_rows // (8 * n_seq)) * 8
    dims = (n_img, n_seq, grid_rows, grid_cols, depth, width, inner)
    vmem = pl.BlockSpec(memory_space=pltpu.VMEM)
    smem = pl.BlockSpec(memory_space=pltpu.SMEM)
    dma = pltpu.SemaphoreType.DMA
    out = pl.pallas_call(
        functools.partial(kernel, dims),
        out_shape=jax.ShapeDtypeStruct((grid_rows, inner, grid_cols), jnp.bfloat16),
        in_specs=[vmem, vmem, smem, smem, vmem],
        out_specs=vmem,
        scratch_shapes=[
            pltpu.VMEM((packed, LANES), jnp.bfloat16),
            pltpu.VMEM((n_img, n_z, packed, LANES), jnp.bfloat16),
            pltpu.VMEM((n_img * (depth // LANES) * LANES, 2 * token_count), jnp.bfloat16),
            pltpu.VMEM((n_img * LANES, 2 * token_count), jnp.bfloat16),
            pltpu.VMEM((n_img * LANES, 2 * token_count), jnp.bfloat16),
            pltpu.VMEM((features, 2 * LANES), jnp.float32),
            pltpu.VMEM((n_z, width, token_count), jnp.float32),
            pltpu.VMEM((3 * inner, token_count), jnp.float32),
            pltpu.VMEM((piece * n_seq, LANES), jnp.float32),
            pltpu.VMEM((n_seq - 1, piece, LANES), jnp.float32),
            pltpu.VMEM((piece * n_seq, LANES), jnp.float32),
            dma((192,)),
            dma((n_img, n_z, 4)),
            dma((2 + n_z,)),
            dma((2 + n_z,)),
            dma((2, n_seq - 1)),
            dma((n_seq - 1,)),
            dma((n_seq - 1,)),
            dma(()),
        ],
        compiler_params=pltpu.CompilerParams(
            collective_id=0, has_side_effects=True, vmem_limit_bytes=56 * 1024 * 1024
        ),
        cost_estimate=pl.CostEstimate(
            flops=2 * token_count * features * 3 * inner, bytes_accessed=4 * token_count * features,
            transcendentals=0,
        ),
    )(
        tokens.transpose(0, 1, 3, 2).reshape(grid_rows, features, grid_cols),
        jnp.stack([norm_gain, caption[0], null_caption]), keep, bucket_rows, w_qkv.T,
    )
    return out.transpose(0, 2, 1).reshape(1, grid_rows, grid_cols, inner)


def body(tokens, norm_gain, caption, null_caption, keep, bucket_rows, w_qkv):
    grid_rows = tokens.shape[1]
    grid_cols = tokens.shape[2]
    features_count = tokens.shape[3]
    token_count = grid_rows * grid_cols
    features = tokens.reshape(token_count, features_count).astype(jnp.float32)
    mean_square = jnp.mean(features * features, axis=1, keepdims=True)
    condition = jnp.where(keep[0] > 0, caption[0], null_caption).astype(jnp.float32)
    hidden = (
        features * lax.rsqrt(mean_square + norm_eps) * norm_gain.astype(jnp.float32) + condition
    ).astype(jnp.bfloat16)
    rows_whole = lax.all_gather(w_qkv, "img", axis=0, tiled=True)
    projected = jnp.dot(
        hidden,
        lax.all_gather(rows_whole, "seq", axis=1, tiled=True),
        preferred_element_type=jnp.float32,
    )
    inner_width = projected.shape[1] // 3
    head_count = inner_width // HDIM
    grid_row = (
        lax.axis_index("seq") * grid_rows + jnp.arange(token_count, dtype=jnp.int32) // grid_cols
    )
    live_mask = (grid_row < bucket_rows[0]).astype(jnp.float32)
    queries = jax.nn.relu(projected[:, :inner_width]).reshape(token_count, head_count, HDIM)
    keys_relu = jax.nn.relu(projected[:, inner_width : 2 * inner_width]).reshape(
        token_count, head_count, HDIM
    )
    keys_relu = keys_relu * live_mask[:, None, None]
    values = projected[:, 2 * inner_width :].reshape(token_count, head_count, HDIM)
    state_outer = jnp.einsum("thd,the->hde", keys_relu, values, precision=lax.Precision.HIGHEST)
    key_total = jnp.sum(keys_relu, axis=0)
    state_outer, key_total = lax.psum((state_outer, key_total), "seq")
    numerator = jnp.einsum("thd,hde->the", queries, state_outer, precision=lax.Precision.HIGHEST)
    denominator = jnp.einsum("thd,hd->th", queries, key_total, precision=lax.Precision.HIGHEST)
    result = numerator / (denominator[:, :, None] + attn_eps) * live_mask[:, None, None]
    return result.reshape(1, grid_rows, grid_cols, inner_width).astype(jnp.bfloat16)


def solution(mesh):
    in_specs = (
        P("img", "seq", None, None),
        P(),
        P("img", None),
        P(),
        P("img"),
        P("img"),
        P("img", "seq"),
    )
    out_specs = P("img", "seq", None, None)
    plane = mesh.shape["img"] == 4 and mesh.shape["seq"] == 8
    run = functools.partial(fast_body, mesh) if plane else body
    return jax.shard_map(run, mesh=mesh, in_specs=in_specs, out_specs=out_specs, check_vma=False)
```
